32 devices in a mesh: ia: 4 (over z), ja: 4 (over y, x), ka: 2 (over core).
Axes of the slice: x: 2, y: 2, z: 4, core: 2. Of those that a mesh axis runs over, the one named last changes fastest.
Arguments:
- tensor: float32 [32, 1024, 1024], P('ka', 'ja', 'ia'), may hold values from -6 to 6
- factor_a: float32 [64, 1024], P('ka', 'ia'), may hold values from -4 to 4
- factor_b: float32 [64, 1024], P('ia', 'ja'), as said below
- factor_c: float32 [64, 32], P('ia', 'ka'), as said below
Outputs:
- gradient: float32 [64, 1024], P('ka', 'ia')
The draws below stay inside these ranges and needn't reach their ends.
Inputs may be any that keep to these rules, and one draw needn't show every extreme that they name: `factor_b`: nonnegative entries. `factor_c`: nonnegative entries.
All inputs are finite; a program needn't handle non-finite values.
Results may differ from the reference program's by a relative error of at most 0.0001.
Values sent between devices are 32-bit elements; how exact they have to be, the bound alone decides.
A program may use at most 64 MiB of HBM per device.

```python
import jax
import jax.numpy as jnp
from jax import lax

R = 64
I = 1024
J = 1024
K = 32


def draw_factor_b(key, part):
    key = jax.random.fold_in(key, 11)
    first = jax.random.fold_in(key, 0)
    values = jax.random.uniform(first, (R, J), jnp.float32) * (3.0 / J) ** 0.5
    return values


def draw_factor_c(key, part):
    key = jax.random.fold_in(key, 23)
    first = jax.random.fold_in(key, 0)
    values = jax.random.uniform(first, (R, K), jnp.float32) * (3.0 / K) ** 0.5
    return values


def block_scale(key, dims, cuts, low, high):
    def one(axis_at, blocks):
        draws = jax.random.uniform(jax.random.fold_in(jax.random.fold_in(key, 6), axis_at), (blocks,), jnp.float32, low / len(cuts), high / len(cuts))
        return jnp.repeat(jnp.exp(draws), dims[axis_at] // blocks).reshape((-1,) + (1,) * (len(dims) - axis_at - 1))

    factor_of = one(*cuts[0])
    for cut in cuts[1:]:
        factor_of = factor_of * one(*cut)
    return factor_of


def bell_draw(key, extent, spread, limit, pieces=(), held_as=jnp.bfloat16):
    gain = block_scale(key, extent, pieces, -0.22, 0.18) if pieces else 1.0
    array = jax.random.normal(key, extent, jnp.float32) * spread * gain
    return jnp.minimum(jnp.maximum(array, -limit), limit).astype(held_as)


def setup_inputs(seed: int = 0) -> dict:
    splits = jax.random.split(jax.random.key(seed), 5)
    return {
        "tensor": bell_draw(splits[0], (K, J, I), 1.0, 6.0, ((0, 2), (1, 4), (2, 4)), jnp.float32),
        "factor_a": bell_draw(splits[1], (R, I), 0.25, 4.0, ((0, 2), (1, 4)), jnp.float32),
        "factor_b": draw_factor_b(jax.random.fold_in(splits[4], 71), 0),
        "factor_c": draw_factor_c(jax.random.fold_in(splits[4], 71), 0),
    }


def reference(tensor, factor_a, factor_b, factor_c):
    highest = lax.Precision.HIGHEST

    def plane_step(total, items):
        plane_slab, column = items
        term = jnp.dot(factor_b, plane_slab, preferred_element_type=jnp.float32, precision=highest)
        return total + term * column[:, None], None

    start_total = jnp.zeros((factor_a.shape[0], tensor.shape[2]), jnp.float32)
    product, unused = lax.scan(plane_step, start_total, (tensor, factor_c.T))
    gram_b = jnp.dot(factor_b, factor_b.T, preferred_element_type=jnp.float32, precision=highest)
    gram_c = jnp.dot(factor_c, factor_c.T, preferred_element_type=jnp.float32, precision=highest)
    hadamard = gram_b * gram_c
    return product - jnp.dot(hadamard, factor_a, preferred_element_type=jnp.float32, precision=highest)
```

```python
import functools

import jax
import jax.numpy as jnp
from jax import lax
from jax.experimental import pallas as pl
from jax.experimental.pallas import tpu as pltpu
from jax.sharding import PartitionSpec as P

MESH = pl.DeviceIdType.MESH
F32 = jnp.float32
BF16 = jnp.bfloat16
NN = (((1,), (0,)), ((), ()))
NT = (((1,), (1,)), ((), ()))


def split(x):
    high = x.astype(BF16)
    return high, (x - high.astype(F32)).astype(BF16)


def dot(x, y, dims=NN):
    return lax.dot_general(x, y, dims, preferred_element_type=F32)


def dot3(x, y, dims=NN):
    xh, xl = split(x)
    yh, yl = split(y)
    return dot(xh, yh, dims) + (dot(xh, yl, dims) + dot(xl, yh, dims))


def kernel(
    n_ia, n_ja, n_ka, groups,
    t_hbm, a_hbm, b_hbm, c_hbm, out_ref,
    t_v, th, tl, pack, c_v, a_v, gc, part, recv,
    t_sem, loc_sem, pack_send, pack_recv, gc_send, gc_recv,
    rs_send, rs_recv, ag_send, ag_recv,
):
    ia, ja, ka = lax.axis_index("ia"), lax.axis_index("ja"), lax.axis_index("ka")
    planes, jl, il = t_v.shape
    rb = pack.shape[1]
    ranks = rb * n_ia
    ra = a_v.shape[1]
    rows = part.shape[1]
    n_red = n_ja * n_ka
    me = ja * n_ka + ka
    step = planes // groups

    own_b = pltpu.make_async_copy(b_hbm, pack.at[ia, :, pl.ds(0, jl)], loc_sem.at[0])
    own_c = pltpu.make_async_copy(c_hbm, c_v, loc_sem.at[1])
    own_b.start()
    own_c.start()
    loads = []
    for g in range(groups):
        load = pltpu.make_async_copy(
            t_hbm.at[pl.ds(g * step, step)], t_v.at[pl.ds(g * step, step)], t_sem.at[g]
        )
        load.start()
        loads.append(load)
    a_v[...] = jnp.zeros_like(a_v)
    own_a = pltpu.make_async_copy(a_hbm, a_v.at[ka], loc_sem.at[2])
    own_a.start()

    barrier = pltpu.get_barrier_semaphore()
    for d in range(1, n_ia):
        pl.semaphore_signal(
            barrier, inc=1, device_id={"ia": lax.rem(ia + d, n_ia)}, device_id_type=MESH
        )
    for d in range(1, n_red):
        peer = lax.rem(me + d, n_red)
        pl.semaphore_signal(
            barrier, inc=1, device_id={"ja": peer // n_ka, "ka": lax.rem(peer, n_ka)},
            device_id_type=MESH,
        )
    own_c.wait()
    pack[ia, :, jl:] = jnp.concatenate(
        [c_v[...], jnp.zeros((rb, pack.shape[2] - jl - planes), F32)], axis=1
    )
    own_b.wait()
    pl.semaphore_wait(barrier, n_ia - 1 + n_red - 1)

    gathers = []
    for d in range(1, n_ia):
        copy = pltpu.make_async_remote_copy(
            src_ref=pack.at[ia], dst_ref=pack.at[ia],
            send_sem=pack_send.at[d - 1], recv_sem=pack_recv.at[ia],
            device_id={"ia": lax.rem(ia + d, n_ia)}, device_id_type=MESH,
        )
        copy.start()
        gathers.append(copy)

    for g in range(groups):
        loads[g].wait()

        @pl.loop(g * step, (g + 1) * step)
        def _(k):
            high, low = split(t_v[k])
            th[k] = high
            tl[k] = low

    for d in range(1, n_ia):
        q = lax.rem(ia + n_ia - d, n_ia)
        pltpu.make_async_remote_copy(
            src_ref=pack.at[q], dst_ref=pack.at[q],
            send_sem=pack_send.at[d - 1], recv_sem=pack_recv.at[q],
            device_id={"ia": q}, device_id_type=MESH,
        ).wait_recv()
    both = jnp.concatenate([pack[q] for q in range(n_ia)], axis=0)
    rank_b = both[:, :jl]
    rank_c = both[:, jl:]

    gc[ka] = dot3(rank_c, rank_c, NT)
    grams = []
    for d in range(1, n_ka):
        copy = pltpu.make_async_remote_copy(
            src_ref=gc.at[ka], dst_ref=gc.at[ka],
            send_sem=gc_send.at[d - 1], recv_sem=gc_recv.at[ka],
            device_id={"ka": lax.rem(ka + d, n_ka)}, device_id_type=MESH,
        )
        copy.start()
        grams.append(copy)

    bh, bl = split(rank_b)
    lhs = jnp.concatenate([bh, bl], axis=0)
    total = jnp.zeros((ranks, il), F32)
    for k in range(planes):
        wide = dot(lhs, th[k])
        inner = wide[:ranks] + (wide[ranks:] + dot(bh, tl[k]))
        total = total + inner * rank_c[:, k : k + 1]
    narrow = dot(lhs, bh, NT)
    gram_b = narrow[:ranks] + (narrow[ranks:] + dot(bh, bl, NT))

    own_a.wait()
    for d in range(1, n_ka):
        q = lax.rem(ka + n_ka - d, n_ka)
        pltpu.make_async_remote_copy(
            src_ref=gc.at[q], dst_ref=gc.at[q],
            send_sem=gc_send.at[d - 1], recv_sem=gc_recv.at[q],
            device_id={"ka": q}, device_id_type=MESH,
        ).wait_recv()
    gram_c = gc[0]
    for q in range(1, n_ka):
        gram_c = gram_c + gc[q]
    share = jnp.concatenate([a_v[q] for q in range(n_ka)], axis=0)
    total = total - dot3(gram_b * gram_c, share)

    for kk in range(n_ka):
        for jj in range(n_ja):
            low = kk * ra + jj * rows
            part[jj * n_ka + kk] = total[low : low + rows]
    scatters = []
    for d in range(1, n_red):
        peer = lax.rem(me + d, n_red)
        copy = pltpu.make_async_remote_copy(
            src_ref=part.at[peer], dst_ref=recv.at[me],
            send_sem=rs_send.at[d - 1], recv_sem=rs_recv.at[me],
            device_id={"ja": peer // n_ka, "ka": lax.rem(peer, n_ka)}, device_id_type=MESH,
        )
        copy.start()
        scatters.append(copy)
    summed = part[me]
    for d in range(1, n_red):
        q = lax.rem(me + n_red - d, n_red)
        pltpu.make_async_remote_copy(
            src_ref=part.at[q], dst_ref=recv.at[q],
            send_sem=rs_send.at[d - 1], recv_sem=rs_recv.at[q],
            device_id={"ja": q // n_ka, "ka": lax.rem(q, n_ka)}, device_id_type=MESH,
        ).wait_recv()
        summed = summed + recv[q]

    out_ref[ja] = summed
    spreads = []
    for d in range(1, n_ja):
        copy = pltpu.make_async_remote_copy(
            src_ref=out_ref.at[ja], dst_ref=out_ref.at[ja],
            send_sem=ag_send.at[d - 1], recv_sem=ag_recv.at[ja],
            device_id={"ja": lax.rem(ja + d, n_ja)}, device_id_type=MESH,
        )
        copy.start()
        spreads.append(copy)
    for copy in gathers + grams + scatters:
        copy.wait_send()
    for d in range(1, n_ja):
        q = lax.rem(ja + n_ja - d, n_ja)
        pltpu.make_async_remote_copy(
            src_ref=out_ref.at[q], dst_ref=out_ref.at[q],
            send_sem=ag_send.at[d - 1], recv_sem=ag_recv.at[q],
            device_id={"ja": q}, device_id_type=MESH,
        ).wait_recv()
    for copy in spreads:
        copy.wait_send()


def local(sizes, tensor, factor_a, factor_b, factor_c):
    n_ia, n_ja, n_ka = sizes
    planes, jl, il = tensor.shape
    ra, rb = factor_a.shape[0], factor_b.shape[0]
    ranks = rb * n_ia
    rows = ra // n_ja
    n_red = n_ja * n_ka
    groups = 4 if planes % 4 == 0 else 1
    wide_c = -(-planes // 128) * 128
    dma = pltpu.SemaphoreType.DMA
    out = pl.pallas_call(
        functools.partial(kernel, n_ia, n_ja, n_ka, groups),
        out_shape=jax.ShapeDtypeStruct((n_ja, rows, il), F32),
        in_specs=[pl.BlockSpec(memory_space=pl.ANY)] * 4,
        out_specs=pl.BlockSpec(memory_space=pltpu.VMEM),
        scratch_shapes=[
            pltpu.VMEM((planes, jl, il), F32),
            pltpu.VMEM((planes, jl, il), BF16),
            pltpu.VMEM((planes, jl, il), BF16),
            pltpu.VMEM((n_ia, rb, jl + wide_c), F32),
            pltpu.VMEM((rb, planes), F32),
            pltpu.VMEM((n_ka, ra, il), F32),
            pltpu.VMEM((n_ka, ranks, ranks), F32),
            pltpu.VMEM((n_red, rows, il), F32),
            pltpu.VMEM((n_red, rows, il), F32),
            dma((groups,)),
            dma((3,)),
            dma((n_ia,)),
            dma((n_ia,)),
            dma((n_ka,)),
            dma((n_ka,)),
            dma((n_red,)),
            dma((n_red,)),
            dma((n_ja,)),
            dma((n_ja,)),
        ],
        compiler_params=pltpu.CompilerParams(
            collective_id=0, has_side_effects=True, vmem_limit_bytes=56 * 2**20
        ),
        cost_estimate=pl.CostEstimate(
            flops=6 * ranks * planes * jl * il,
            bytes_accessed=4 * planes * jl * il,
            transcendentals=0,
        ),
    )(tensor, factor_a, factor_b, factor_c)
    return out.reshape(ra, il)


def solution(mesh):
    sizes = tuple(mesh.shape[name] for name in ("ia", "ja", "ka"))
    in_specs = (P("ka", "ja", "ia"), P("ka", "ia"), P("ia", "ja"), P("ia", "ka"))
    return jax.shard_map(
        functools.partial(local, sizes), mesh=mesh, in_specs=in_specs,
        out_specs=P("ka", "ia"), check_vma=False,
    )
```

```python
import functools

import jax
import jax.numpy as jnp
from jax import lax
from jax.experimental import pallas as pl
from jax.experimental.pallas import tpu as pltpu
from jax.sharding import PartitionSpec as P

MESH = pl.DeviceIdType.MESH
F32 = jnp.float32
BF16 = jnp.bfloat16
NN = (((1,), (0,)), ((), ()))
NT = (((1,), (1,)), ((), ()))


def split(x):
    high = x.astype(BF16)
    return high, (x - high.astype(F32)).astype(BF16)


def dot(x, y, dims=NN):
    return lax.dot_general(x, y, dims, preferred_element_type=F32)


def dot3(x, y, dims=NN):
    xh, xl = split(x)
    yh, yl = split(y)
    return dot(xh, yh, dims) + (dot(xh, yl, dims) + dot(xl, yh, dims))


def kernel(
    n_ia, n_ja, n_ka, groups,
    t_hbm, a_hbm, b_hbm, c_hbm, out_ref,
    t_v, th, tl, pack, c_v, a_v, gc, part, recv,
    t_sem, loc_sem, pack_send, pack_recv, gc_send, gc_recv,
    rs_send, rs_recv, ag_send, ag_recv,
):
    ia, ja, ka = lax.axis_index("ia"), lax.axis_index("ja"), lax.axis_index("ka")
    planes, jl, il = t_v.shape
    rb = pack.shape[1]
    ranks = rb * n_ia
    ra = a_v.shape[1]
    rows = part.shape[1]
    n_red = n_ja * n_ka
    me = ja * n_ka + ka
    step = planes // groups

    own_b = pltpu.make_async_copy(b_hbm, pack.at[ia, :, pl.ds(0, jl)], loc_sem.at[0])
    own_c = pltpu.make_async_copy(c_hbm, c_v, loc_sem.at[1])
    own_b.start()
    own_c.start()
    loads = []
    for g in range(groups):
        load = pltpu.make_async_copy(
            t_hbm.at[pl.ds(g * step, step)], t_v.at[pl.ds(g * step, step)], t_sem.at[g]
        )
        load.start()
        loads.append(load)
    a_v[...] = jnp.zeros_like(a_v)
    own_a = pltpu.make_async_copy(a_hbm, a_v.at[ka], loc_sem.at[2])
    own_a.start()

    barrier = pltpu.get_barrier_semaphore()
    for d in range(1, n_ia):
        pl.semaphore_signal(
            barrier, inc=1, device_id={"ia": lax.rem(ia + d, n_ia)}, device_id_type=MESH
        )
    for d in range(1, n_red):
        peer = lax.rem(me + d, n_red)
        pl.semaphore_signal(
            barrier, inc=1, device_id={"ja": peer // n_ka, "ka": lax.rem(peer, n_ka)},
            device_id_type=MESH,
        )
    own_c.wait()
    pack[ia, :, jl:] = jnp.concatenate(
        [c_v[...], jnp.zeros((rb, pack.shape[2] - jl - planes), F32)], axis=1
    )
    own_b.wait()
    pl.semaphore_wait(barrier, n_ia - 1 + n_red - 1)

    gathers = []
    for d in range(1, n_ia):
        copy = pltpu.make_async_remote_copy(
            src_ref=pack.at[ia], dst_ref=pack.at[ia],
            send_sem=pack_send.at[d - 1], recv_sem=pack_recv.at[ia],
            device_id={"ia": lax.rem(ia + d, n_ia)}, device_id_type=MESH,
        )
        copy.start()
        gathers.append(copy)

    early = groups // 2
    for g in range(early):
        loads[g].wait()

        @pl.loop(g * step, (g + 1) * step)
        def _(k):
            high, low = split(t_v[k])
            th[k] = high
            tl[k] = low

    for d in range(1, n_ia):
        q = lax.rem(ia + n_ia - d, n_ia)
        pltpu.make_async_remote_copy(
            src_ref=pack.at[q], dst_ref=pack.at[q],
            send_sem=pack_send.at[d - 1], recv_sem=pack_recv.at[q],
            device_id={"ia": q}, device_id_type=MESH,
        ).wait_recv()
    both = jnp.concatenate([pack[q] for q in range(n_ia)], axis=0)
    rank_b = both[:, :jl]
    rank_c = both[:, jl:]

    gc[ka] = dot3(rank_c, rank_c, NT)
    grams = []
    for d in range(1, n_ka):
        copy = pltpu.make_async_remote_copy(
            src_ref=gc.at[ka], dst_ref=gc.at[ka],
            send_sem=gc_send.at[d - 1], recv_sem=gc_recv.at[ka],
            device_id={"ka": lax.rem(ka + d, n_ka)}, device_id_type=MESH,
        )
        copy.start()
        grams.append(copy)

    bh, bl = split(rank_b)
    lhs = jnp.concatenate([bh, bl], axis=0)

    def planes_of(g, total):
        for k in range(g * step, (g + 1) * step):
            if g < early:
                high, low = th[k], tl[k]
            else:
                high, low = split(t_v[k])
            wide = dot(lhs, high)
            inner = wide[:ranks] + (wide[ranks:] + dot(bh, low))
            total = total + inner * rank_c[:, k : k + 1]
        return total

    total = jnp.zeros((ranks, il), F32)
    for g in range(early):
        total = planes_of(g, total)
    narrow = dot(lhs, bh, NT)
    gram_b = narrow[:ranks] + (narrow[ranks:] + dot(bh, bl, NT))

    own_a.wait()
    for load in loads[early:]:
        load.wait()
    for d in range(1, n_ka):
        q = lax.rem(ka + n_ka - d, n_ka)
        pltpu.make_async_remote_copy(
            src_ref=gc.at[q], dst_ref=gc.at[q],
            send_sem=gc_send.at[d - 1], recv_sem=gc_recv.at[q],
            device_id={"ka": q}, device_id_type=MESH,
        ).wait_recv()
    gram_c = gc[0]
    for q in range(1, n_ka):
        gram_c = gram_c + gc[q]
    share = jnp.concatenate([a_v[q] for q in range(n_ka)], axis=0)
    total = total - dot3(gram_b * gram_c, share)
    for g in range(early, groups):
        total = planes_of(g, total)

    for kk in range(n_ka):
        for jj in range(n_ja):
            low = kk * ra + jj * rows
            part[jj * n_ka + kk] = total[low : low + rows]
    scatters = []
    for d in range(1, n_red):
        peer = lax.rem(me + d, n_red)
        copy = pltpu.make_async_remote_copy(
            src_ref=part.at[peer], dst_ref=recv.at[me],
            send_sem=rs_send.at[d - 1], recv_sem=rs_recv.at[me],
            device_id={"ja": peer // n_ka, "ka": lax.rem(peer, n_ka)}, device_id_type=MESH,
        )
        copy.start()
        scatters.append(copy)
    summed = part[me]
    for d in range(1, n_red):
        q = lax.rem(me + n_red - d, n_red)
        pltpu.make_async_remote_copy(
            src_ref=part.at[q], dst_ref=recv.at[q],
            send_sem=rs_send.at[d - 1], recv_sem=rs_recv.at[q],
            device_id={"ja": q // n_ka, "ka": lax.rem(q, n_ka)}, device_id_type=MESH,
        ).wait_recv()
        summed = summed + recv[q]

    out_ref[ja] = summed
    spreads = []
    for d in range(1, n_ja):
        copy = pltpu.make_async_remote_copy(
            src_ref=out_ref.at[ja], dst_ref=out_ref.at[ja],
            send_sem=ag_send.at[d - 1], recv_sem=ag_recv.at[ja],
            device_id={"ja": lax.rem(ja + d, n_ja)}, device_id_type=MESH,
        )
        copy.start()
        spreads.append(copy)
    for copy in gathers + grams + scatters:
        copy.wait_send()
    for d in range(1, n_ja):
        q = lax.rem(ja + n_ja - d, n_ja)
        pltpu.make_async_remote_copy(
            src_ref=out_ref.at[q], dst_ref=out_ref.at[q],
            send_sem=ag_send.at[d - 1], recv_sem=ag_recv.at[q],
            device_id={"ja": q}, device_id_type=MESH,
        ).wait_recv()
    for copy in spreads:
        copy.wait_send()


def local(sizes, tensor, factor_a, factor_b, factor_c):
    n_ia, n_ja, n_ka = sizes
    planes, jl, il = tensor.shape
    ra, rb = factor_a.shape[0], factor_b.shape[0]
    ranks = rb * n_ia
    rows = ra // n_ja
    n_red = n_ja * n_ka
    groups = 4
    wide_c = -(-planes // 128) * 128
    dma = pltpu.SemaphoreType.DMA
    out = pl.pallas_call(
        functools.partial(kernel, n_ia, n_ja, n_ka, groups),
        out_shape=pltpu.VMEM((n_ja, rows, il), F32),
        in_specs=[pl.BlockSpec(memory_space=pl.ANY)] * 4,
        out_specs=pl.BlockSpec(memory_space=pltpu.VMEM),
        scratch_shapes=[
            pltpu.VMEM((planes, jl, il), F32),
            pltpu.VMEM((planes // 2, jl, il), BF16),
            pltpu.VMEM((planes // 2, jl, il), BF16),
            pltpu.VMEM((n_ia, rb, jl + wide_c), F32),
            pltpu.VMEM((rb, planes), F32),
            pltpu.VMEM((n_ka, ra, il), F32),
            pltpu.VMEM((n_ka, ranks, ranks), F32),
            pltpu.VMEM((n_red, rows, il), F32),
            pltpu.VMEM((n_red, rows, il), F32),
            dma((groups,)),
            dma((3,)),
            dma((n_ia,)),
            dma((n_ia,)),
            dma((n_ka,)),
            dma((n_ka,)),
            dma((n_red,)),
            dma((n_red,)),
            dma((n_ja,)),
            dma((n_ja,)),
        ],
        compiler_params=pltpu.CompilerParams(
            collective_id=0, has_side_effects=True, vmem_limit_bytes=56 * 2**20
        ),
        cost_estimate=pl.CostEstimate(
            flops=6 * ranks * planes * jl * il,
            bytes_accessed=4 * planes * jl * il,
            transcendentals=0,
        ),
    )(tensor, factor_a, factor_b, factor_c)
    return out.reshape(ra, il)


def solution(mesh):
    sizes = tuple(mesh.shape[name] for name in ("ia", "ja", "ka"))
    in_specs = (P("ka", "ja", "ia"), P("ka", "ia"), P("ia", "ja"), P("ia", "ka"))
    return jax.shard_map(
        functools.partial(local, sizes), mesh=mesh, in_specs=in_specs,
        out_specs=P("ka", "ia"), check_vma=False,
    )
```

```python
import functools

import jax
import jax.numpy as jnp
from jax import lax
from jax.experimental import pallas as pl
from jax.experimental.pallas import tpu as pltpu
from jax.sharding import PartitionSpec as P

MESH = pl.DeviceIdType.MESH
F32 = jnp.float32
BF16 = jnp.bfloat16
NN = (((1,), (0,)), ((), ()))
NT = (((1,), (1,)), ((), ()))


def split(x):
    high = x.astype(BF16)
    return high, (x - high.astype(F32)).astype(BF16)


def dot(x, y, dims=NN):
    return lax.dot_general(x, y, dims, preferred_element_type=F32)


def dot3(x, y, dims=NN):
    xh, xl = split(x)
    yh, yl = split(y)
    return dot(xh, yh, dims) + (dot(xh, yl, dims) + dot(xl, yh, dims))


def kernel(
    n_ia, n_ja, n_ka, groups,
    t_hbm, a_hbm, b_hbm, c_hbm, out_ref,
    t_v, th, tl, pack, c_v, a_v, gc, part, recv,
    t_sem, loc_sem, up_send, pack_send, pack_recv, gc_send, gc_recv,
    rs_send, rs_recv, ag_send, ag_recv,
):
    ia, ja, ka = lax.axis_index("ia"), lax.axis_index("ja"), lax.axis_index("ka")
    planes, jl, il = t_v.shape
    rb = pack.shape[1]
    ranks = rb * n_ia
    ra = a_v.shape[1]
    rows = part.shape[1]
    n_red = n_ja * n_ka
    me = ja * n_ka + ka
    step = planes // groups

    barrier = pltpu.get_barrier_semaphore()
    for q in range(n_ia):

        @pl.when((q > ia) | (q == ia - 1))
        def _():
            pl.semaphore_signal(barrier, inc=1, device_id={"ia": q}, device_id_type=MESH)

    for d in range(1, n_red):
        peer = lax.rem(me + d, n_red)
        pl.semaphore_signal(
            barrier, inc=1, device_id={"ja": peer // n_ka, "ka": lax.rem(peer, n_ka)},
            device_id_type=MESH,
        )

    own_b = pltpu.make_async_copy(b_hbm, pack.at[ia, :, pl.ds(0, jl)], loc_sem.at[0])
    own_c = pltpu.make_async_copy(c_hbm, c_v, loc_sem.at[1])
    own_b.start()
    own_c.start()
    loads = []
    for g in range(groups):
        load = pltpu.make_async_copy(
            t_hbm.at[pl.ds(g * step, step)], t_v.at[pl.ds(g * step, step)], t_sem.at[g]
        )
        load.start()
        loads.append(load)
    a_v[...] = jnp.zeros_like(a_v)
    own_a = pltpu.make_async_copy(a_hbm, a_v.at[ka], loc_sem.at[2])
    own_a.start()
    own_c.wait()
    pack[ia, :, jl:] = jnp.concatenate(
        [c_v[...], jnp.zeros((rb, pack.shape[2] - jl - planes), F32)], axis=1
    )
    own_b.wait()
    pl.semaphore_wait(barrier, n_red - 1 + ia + jnp.where(ia < n_ia - 1, 1, 0))

    def passed(slot, to, sem):
        return pltpu.make_async_remote_copy(
            src_ref=pack.at[slot], dst_ref=pack.at[slot],
            send_sem=sem, recv_sem=pack_recv.at[slot],
            device_id={"ia": to}, device_id_type=MESH,
        )

    def upward(slot):
        return passed(slot, lax.rem(ia + 1, n_ia), up_send.at[slot])

    def downward(to):
        return passed(ia, to, pack_send.at[to])

    @pl.when(ia < n_ia - 1)
    def _():
        upward(ia).start()

    for q in range(n_ia - 1):

        @pl.when(q < ia)
        def _():
            downward(q).start()

    for q in reversed(range(n_ia - 1)):

        @pl.when(q < ia)
        def _():
            passed(q, q, pack_send.at[q]).wait_recv()

        @pl.when((q < ia) & (ia < n_ia - 1))
        def _():
            upward(q).start()

    early = groups // 2
    for g in range(early):
        loads[g].wait()

        @pl.loop(g * step, (g + 1) * step)
        def _(k):
            high, low = split(t_v[k])
            th[k] = high
            tl[k] = low

    for q in range(1, n_ia):

        @pl.when(q > ia)
        def _():
            passed(q, q, pack_send.at[q]).wait_recv()

    both = jnp.concatenate([pack[q] for q in range(n_ia)], axis=0)
    rank_b = both[:, :jl]
    rank_c = both[:, jl:]

    bh, bl = split(rank_b)
    lhs = jnp.concatenate([bh, bl], axis=0)

    def planes_of(g, total):
        for k in range(g * step, (g + 1) * step):
            if g < early:
                high, low = th[k], tl[k]
            else:
                high, low = split(t_v[k])
            wide = dot(lhs, high)
            inner = wide[:ranks] + (wide[ranks:] + dot(bh, low))
            total = total + inner * rank_c[:, k : k + 1]
        return total

    total = jnp.zeros((ranks, il), F32)
    total = planes_of(0, total)

    gc[ka] = dot3(rank_c, rank_c, NT)
    grams = []
    for d in range(1, n_ka):
        copy = pltpu.make_async_remote_copy(
            src_ref=gc.at[ka], dst_ref=gc.at[ka],
            send_sem=gc_send.at[d - 1], recv_sem=gc_recv.at[ka],
            device_id={"ka": lax.rem(ka + d, n_ka)}, device_id_type=MESH,
        )
        copy.start()
        grams.append(copy)

    for g in range(1, early):
        total = planes_of(g, total)
    narrow = dot(lhs, bh, NT)
    gram_b = narrow[:ranks] + (narrow[ranks:] + dot(bh, bl, NT))

    own_a.wait()
    for load in loads[early:]:
        load.wait()
    for d in range(1, n_ka):
        q = lax.rem(ka + n_ka - d, n_ka)
        pltpu.make_async_remote_copy(
            src_ref=gc.at[q], dst_ref=gc.at[q],
            send_sem=gc_send.at[d - 1], recv_sem=gc_recv.at[q],
            device_id={"ka": q}, device_id_type=MESH,
        ).wait_recv()
    gram_c = gc[0]
    for q in range(1, n_ka):
        gram_c = gram_c + gc[q]
    share = jnp.concatenate([a_v[q] for q in range(n_ka)], axis=0)
    total = total - dot3(gram_b * gram_c, share)
    for g in range(early, groups):
        total = planes_of(g, total)

    for kk in range(n_ka):
        for jj in range(n_ja):
            low = kk * ra + jj * rows
            part[jj * n_ka + kk] = total[low : low + rows]
    scatters = []
    for d in range(1, n_red):
        peer = lax.rem(me + d, n_red)
        copy = pltpu.make_async_remote_copy(
            src_ref=part.at[peer], dst_ref=recv.at[me],
            send_sem=rs_send.at[d - 1], recv_sem=rs_recv.at[me],
            device_id={"ja": peer // n_ka, "ka": lax.rem(peer, n_ka)}, device_id_type=MESH,
        )
        copy.start()
        scatters.append(copy)
    summed = part[me]
    for d in range(1, n_red):
        q = lax.rem(me + n_red - d, n_red)
        pltpu.make_async_remote_copy(
            src_ref=part.at[q], dst_ref=recv.at[q],
            send_sem=rs_send.at[d - 1], recv_sem=rs_recv.at[q],
            device_id={"ja": q // n_ka, "ka": lax.rem(q, n_ka)}, device_id_type=MESH,
        ).wait_recv()
        summed = summed + recv[q]

    out_ref[ja] = summed
    spreads = []
    for d in range(1, n_ja):
        copy = pltpu.make_async_remote_copy(
            src_ref=out_ref.at[ja], dst_ref=out_ref.at[ja],
            send_sem=ag_send.at[d - 1], recv_sem=ag_recv.at[ja],
            device_id={"ja": lax.rem(ja + d, n_ja)}, device_id_type=MESH,
        )
        copy.start()
        spreads.append(copy)
    for copy in grams + scatters:
        copy.wait_send()
    for q in range(n_ia - 1):

        @pl.when(q < ia)
        def _():
            downward(q).wait_send()

        @pl.when((q <= ia) & (ia < n_ia - 1))
        def _():
            upward(q).wait_send()

    for d in range(1, n_ja):
        q = lax.rem(ja + n_ja - d, n_ja)
        pltpu.make_async_remote_copy(
            src_ref=out_ref.at[q], dst_ref=out_ref.at[q],
            send_sem=ag_send.at[d - 1], recv_sem=ag_recv.at[q],
            device_id={"ja": q}, device_id_type=MESH,
        ).wait_recv()
    for copy in spreads:
        copy.wait_send()


def local(sizes, tensor, factor_a, factor_b, factor_c):
    n_ia, n_ja, n_ka = sizes
    planes, jl, il = tensor.shape
    ra, rb = factor_a.shape[0], factor_b.shape[0]
    ranks = rb * n_ia
    rows = ra // n_ja
    n_red = n_ja * n_ka
    groups = 4
    wide_c = -(-planes // 128) * 128
    dma = pltpu.SemaphoreType.DMA
    out = pl.pallas_call(
        functools.partial(kernel, n_ia, n_ja, n_ka, groups),
        out_shape=pltpu.VMEM((n_ja, rows, il), F32),
        in_specs=[pl.BlockSpec(memory_space=pl.ANY)] * 4,
        out_specs=pl.BlockSpec(memory_space=pltpu.VMEM),
        scratch_shapes=[
            pltpu.VMEM((planes, jl, il), F32),
            pltpu.VMEM((planes // 2, jl, il), BF16),
            pltpu.VMEM((planes // 2, jl, il), BF16),
            pltpu.VMEM((n_ia, rb, jl + wide_c), F32),
            pltpu.VMEM((rb, planes), F32),
            pltpu.VMEM((n_ka, ra, il), F32),
            pltpu.VMEM((n_ka, ranks, ranks), F32),
            pltpu.VMEM((n_red, rows, il), F32),
            pltpu.VMEM((n_red, rows, il), F32),
            dma((groups,)),
            dma((3,)),
            dma((n_ia,)),
            dma((n_ia,)),
            dma((n_ia,)),
            dma((n_ka,)),
            dma((n_ka,)),
            dma((n_red,)),
            dma((n_red,)),
            dma((n_ja,)),
            dma((n_ja,)),
        ],
        compiler_params=pltpu.CompilerParams(
            collective_id=0, has_side_effects=True, vmem_limit_bytes=56 * 2**20
        ),
        cost_estimate=pl.CostEstimate(
            flops=6 * ranks * planes * jl * il,
            bytes_accessed=4 * planes * jl * il,
            transcendentals=0,
        ),
    )(tensor, factor_a, factor_b, factor_c)
    return out.reshape(ra, il)


def solution(mesh):
    sizes = tuple(mesh.shape[name] for name in ("ia", "ja", "ka"))
    in_specs = (P("ka", "ja", "ia"), P("ka", "ia"), P("ia", "ja"), P("ia", "ka"))
    return jax.shard_map(
        functools.partial(local, sizes), mesh=mesh, in_specs=in_specs,
        out_specs=P("ka", "ia"), check_vma=False,
    )
```

```python
import functools

import jax
import jax.numpy as jnp
from jax import lax
from jax.experimental import pallas as pl
from jax.experimental.pallas import tpu as pltpu
from jax.sharding import PartitionSpec as P

MESH = pl.DeviceIdType.MESH
F32 = jnp.float32
BF16 = jnp.bfloat16
NN = (((1,), (0,)), ((), ()))
NT = (((1,), (1,)), ((), ()))


def split(x):
    high = x.astype(BF16)
    return high, (x - high.astype(F32)).astype(BF16)


def dot(x, y, dims=NN):
    return lax.dot_general(x, y, dims, preferred_element_type=F32)


def dot3(x, y, dims=NN):
    xh, xl = split(x)
    yh, yl = split(y)
    return dot(xh, yh, dims) + (dot(xh, yl, dims) + dot(xl, yh, dims))


def kernel(
    n_ia, n_ja, n_ka, groups,
    t_hbm, a_hbm, b_hbm, c_hbm, out_ref,
    t_v, th, tl, pack, c_v, a_v, gc, part, recv,
    t_sem, loc_sem, pack_send, pack_recv, gc_send, gc_recv,
    rs_send, rs_recv, ag_send, ag_recv,
):
    ia, ja, ka = lax.axis_index("ia"), lax.axis_index("ja"), lax.axis_index("ka")
    planes, jl, il = t_v.shape
    rb = pack.shape[1]
    ranks = rb * n_ia
    ra = a_v.shape[1]
    rows = part.shape[1]
    n_red = n_ja * n_ka
    me = ja * n_ka + ka
    step = planes // groups

    barrier = pltpu.get_barrier_semaphore()
    for d in range(1, n_ia):
        pl.semaphore_signal(
            barrier, inc=1, device_id={"ia": lax.rem(ia + d, n_ia)}, device_id_type=MESH
        )
    for d in range(1, n_red):
        peer = lax.rem(me + d, n_red)
        pl.semaphore_signal(
            barrier, inc=1, device_id={"ja": peer // n_ka, "ka": lax.rem(peer, n_ka)},
            device_id_type=MESH,
        )
    own_b = pltpu.make_async_copy(b_hbm, pack.at[ia, :, pl.ds(0, jl)], loc_sem.at[0])
    own_c = pltpu.make_async_copy(c_hbm, c_v, loc_sem.at[1])
    own_b.start()
    own_c.start()
    loads = []
    for g in range(groups):
        load = pltpu.make_async_copy(
            t_hbm.at[pl.ds(g * step, step)], t_v.at[pl.ds(g * step, step)], t_sem.at[g]
        )
        load.start()
        loads.append(load)
    a_v[...] = jnp.zeros_like(a_v)
    own_a = pltpu.make_async_copy(a_hbm, a_v.at[ka], loc_sem.at[2])
    own_a.start()

    own_c.wait()
    pack[ia, :, jl:] = jnp.concatenate(
        [c_v[...], jnp.zeros((rb, pack.shape[2] - jl - planes), F32)], axis=1
    )
    own_b.wait()
    pl.semaphore_wait(barrier, n_ia - 1 + n_red - 1)

    gathers = []
    for d in range(1, n_ia):
        copy = pltpu.make_async_remote_copy(
            src_ref=pack.at[ia], dst_ref=pack.at[ia],
            send_sem=pack_send.at[d - 1], recv_sem=pack_recv.at[ia],
            device_id={"ia": lax.rem(ia + d, n_ia)}, device_id_type=MESH,
        )
        copy.start()
        gathers.append(copy)

    for g in range(groups):
        loads[g].wait()

        @pl.loop(g * step, (g + 1) * step)
        def _(k):
            high, low = split(t_v[k])
            th[k] = high
            tl[k] = low

    for d in range(1, n_ia):
        q = lax.rem(ia + n_ia - d, n_ia)
        pltpu.make_async_remote_copy(
            src_ref=pack.at[q], dst_ref=pack.at[q],
            send_sem=pack_send.at[d - 1], recv_sem=pack_recv.at[q],
            device_id={"ia": q}, device_id_type=MESH,
        ).wait_recv()
    both = jnp.concatenate([pack[q] for q in range(n_ia)], axis=0)
    rank_b = both[:, :jl]
    rank_c = both[:, jl:]

    gc[ka] = dot3(rank_c, rank_c, NT)
    grams = []
    for d in range(1, n_ka):
        copy = pltpu.make_async_remote_copy(
            src_ref=gc.at[ka], dst_ref=gc.at[ka],
            send_sem=gc_send.at[d - 1], recv_sem=gc_recv.at[ka],
            device_id={"ka": lax.rem(ka + d, n_ka)}, device_id_type=MESH,
        )
        copy.start()
        grams.append(copy)

    bh, bl = split(rank_b)
    lhs = jnp.concatenate([bh, bl], axis=0)
    lane = lax.broadcasted_iota(jnp.int32, rank_c.shape, 1)

    def planes_of(g, total):
        for u in range(step):
            k = g * step + u
            column = jnp.sum(jnp.where(lane == k, rank_c, 0.0), axis=1, keepdims=True)
            wide = dot(lhs, th[k])
            inner = wide[:ranks] + (wide[ranks:] + dot(bh, tl[k]))
            total = total + inner * column
        return total

    total = lax.fori_loop(0, groups - 1, planes_of, jnp.zeros((ranks, il), F32))

    narrow = dot(lhs, bh, NT)
    gram_b = narrow[:ranks] + (narrow[ranks:] + dot(bh, bl, NT))
    own_a.wait()
    for d in range(1, n_ka):
        q = lax.rem(ka + n_ka - d, n_ka)
        pltpu.make_async_remote_copy(
            src_ref=gc.at[q], dst_ref=gc.at[q],
            send_sem=gc_send.at[d - 1], recv_sem=gc_recv.at[q],
            device_id={"ka": q}, device_id_type=MESH,
        ).wait_recv()
    gram_c = gc[0]
    for q in range(1, n_ka):
        gram_c = gram_c + gc[q]
    share = jnp.concatenate([a_v[q] for q in range(n_ka)], axis=0)
    total = total - dot3(gram_b * gram_c, share)
    total = planes_of(groups - 1, total)

    for kk in range(n_ka):
        for jj in range(n_ja):
            low = kk * ra + jj * rows
            part[jj * n_ka + kk] = total[low : low + rows]
    scatters = []
    for d in range(1, n_red):
        peer = lax.rem(me + d, n_red)
        copy = pltpu.make_async_remote_copy(
            src_ref=part.at[peer], dst_ref=recv.at[me],
            send_sem=rs_send.at[d - 1], recv_sem=rs_recv.at[me],
            device_id={"ja": peer // n_ka, "ka": lax.rem(peer, n_ka)}, device_id_type=MESH,
        )
        copy.start()
        scatters.append(copy)
    summed = part[me]
    for d in range(1, n_red):
        q = lax.rem(me + n_red - d, n_red)
        pltpu.make_async_remote_copy(
            src_ref=part.at[q], dst_ref=recv.at[q],
            send_sem=rs_send.at[d - 1], recv_sem=rs_recv.at[q],
            device_id={"ja": q // n_ka, "ka": lax.rem(q, n_ka)}, device_id_type=MESH,
        ).wait_recv()
        summed = summed + recv[q]

    out_ref[ja] = summed
    spreads = []
    for d in range(1, n_ja):
        copy = pltpu.make_async_remote_copy(
            src_ref=out_ref.at[ja], dst_ref=out_ref.at[ja],
            send_sem=ag_send.at[d - 1], recv_sem=ag_recv.at[ja],
            device_id={"ja": lax.rem(ja + d, n_ja)}, device_id_type=MESH,
        )
        copy.start()
        spreads.append(copy)
    for copy in gathers + grams + scatters:
        copy.wait_send()
    for d in range(1, n_ja):
        q = lax.rem(ja + n_ja - d, n_ja)
        pltpu.make_async_remote_copy(
            src_ref=out_ref.at[q], dst_ref=out_ref.at[q],
            send_sem=ag_send.at[d - 1], recv_sem=ag_recv.at[q],
            device_id={"ja": q}, device_id_type=MESH,
        ).wait_recv()
    for copy in spreads:
        copy.wait_send()


def local(sizes, tensor, factor_a, factor_b, factor_c):
    n_ia, n_ja, n_ka = sizes
    planes, jl, il = tensor.shape
    ra, rb = factor_a.shape[0], factor_b.shape[0]
    ranks = rb * n_ia
    rows = ra // n_ja
    n_red = n_ja * n_ka
    groups = 4
    wide_c = -(-planes // 128) * 128
    dma = pltpu.SemaphoreType.DMA
    out = pl.pallas_call(
        functools.partial(kernel, n_ia, n_ja, n_ka, groups),
        out_shape=pltpu.VMEM((n_ja, rows, il), F32),
        in_specs=[pl.BlockSpec(memory_space=pl.ANY)] * 4,
        out_specs=pl.BlockSpec(memory_space=pltpu.VMEM),
        scratch_shapes=[
            pltpu.VMEM((planes, jl, il), F32),
            pltpu.VMEM((planes, jl, il), BF16),
            pltpu.VMEM((planes, jl, il), BF16),
            pltpu.VMEM((n_ia, rb, jl + wide_c), F32),
            pltpu.VMEM((rb, planes), F32),
            pltpu.VMEM((n_ka, ra, il), F32),
            pltpu.VMEM((n_ka, ranks, ranks), F32),
            pltpu.VMEM((n_red, rows, il), F32),
            pltpu.VMEM((n_red, rows, il), F32),
            dma((groups,)),
            dma((3,)),
            dma((n_ia,)),
            dma((n_ia,)),
            dma((n_ka,)),
            dma((n_ka,)),
            dma((n_red,)),
            dma((n_red,)),
            dma((n_ja,)),
            dma((n_ja,)),
        ],
        compiler_params=pltpu.CompilerParams(
            collective_id=0, has_side_effects=True, vmem_limit_bytes=56 * 2**20
        ),
        cost_estimate=pl.CostEstimate(
            flops=6 * ranks * planes * jl * il,
            bytes_accessed=4 * planes * jl * il,
            transcendentals=0,
        ),
    )(tensor, factor_a, factor_b, factor_c)
    return out.reshape(ra, il)


def solution(mesh):
    sizes = tuple(mesh.shape[name] for name in ("ia", "ja", "ka"))
    in_specs = (P("ka", "ja", "ia"), P("ka", "ia"), P("ia", "ja"), P("ia", "ka"))
    return jax.shard_map(
        functools.partial(local, sizes), mesh=mesh, in_specs=in_specs,
        out_specs=P("ka", "ia"), check_vma=False,
    )
```

```python
import functools

import jax
import jax.numpy as jnp
from jax import lax
from jax.experimental import pallas as pl
from jax.experimental.pallas import tpu as pltpu
from jax.sharding import PartitionSpec as P

MESH = pl.DeviceIdType.MESH
F32 = jnp.float32
BF16 = jnp.bfloat16
NN = (((1,), (0,)), ((), ()))
NT = (((1,), (1,)), ((), ()))


def split(x):
    high = x.astype(BF16)
    return high, (x - high.astype(F32)).astype(BF16)


def dot(x, y, dims=NN):
    return lax.dot_general(x, y, dims, preferred_element_type=F32)


def dot3(x, y, dims=NN):
    xh, xl = split(x)
    yh, yl = split(y)
    return dot(xh, yh, dims) + (dot(xh, yl, dims) + dot(xl, yh, dims))


def kernel(
    n_ia, n_ja, n_ka, groups,
    t_hbm, a_hbm, b_hbm, c_hbm, out_ref,
    t_v, th, tl, pack, c_v, a_v, gc, part, recv,
    t_sem, loc_sem, pack_send, pack_recv, gc_send, gc_recv,
    rs_send, rs_recv, ag_send, ag_recv,
):
    ia, ja, ka = lax.axis_index("ia"), lax.axis_index("ja"), lax.axis_index("ka")
    planes, jl, il = t_v.shape
    rb = pack.shape[1]
    ranks = rb * n_ia
    ra = a_v.shape[1]
    rows = part.shape[1]
    n_red = n_ja * n_ka
    me = ja * n_ka + ka
    step = planes // groups

    barrier = pltpu.get_barrier_semaphore()
    for d in range(1, n_ia):
        pl.semaphore_signal(
            barrier, inc=1, device_id={"ia": lax.rem(ia + d, n_ia)}, device_id_type=MESH
        )
    @pl.loop(1, n_red)
    def _(d):
        peer = lax.rem(me + d, n_red)
        pl.semaphore_signal(
            barrier, inc=1, device_id={"ja": peer // n_ka, "ka": lax.rem(peer, n_ka)},
            device_id_type=MESH,
        )
    own_b = pltpu.make_async_copy(b_hbm, pack.at[ia, :, pl.ds(0, jl)], loc_sem.at[0])
    own_c = pltpu.make_async_copy(c_hbm, c_v, loc_sem.at[1])
    own_b.start()
    own_c.start()
    loads = []
    for g in range(groups):
        load = pltpu.make_async_copy(
            t_hbm.at[pl.ds(g * step, step)], t_v.at[pl.ds(g * step, step)], t_sem.at[g]
        )
        load.start()
        loads.append(load)
    a_v[...] = jnp.zeros_like(a_v)
    own_a = pltpu.make_async_copy(a_hbm, a_v.at[ka], loc_sem.at[2])
    own_a.start()

    own_c.wait()
    pack[ia, :, jl:] = jnp.concatenate(
        [c_v[...], jnp.zeros((rb, pack.shape[2] - jl - planes), F32)], axis=1
    )
    own_b.wait()
    pl.semaphore_wait(barrier, n_ia - 1 + n_red - 1)

    gathers = []
    for d in range(1, n_ia):
        copy = pltpu.make_async_remote_copy(
            src_ref=pack.at[ia], dst_ref=pack.at[ia],
            send_sem=pack_send.at[d - 1], recv_sem=pack_recv.at[ia],
            device_id={"ia": lax.rem(ia + d, n_ia)}, device_id_type=MESH,
        )
        copy.start()
        gathers.append(copy)

    for g in range(groups):
        loads[g].wait()

        @pl.loop(g * step, (g + 1) * step)
        def _(k):
            high, low = split(t_v[k])
            columns = pl.ds(pl.multiple_of(k * il, il), il)
            th[:, columns] = high
            tl[:, columns] = low

    for d in range(1, n_ia):
        q = lax.rem(ia + n_ia - d, n_ia)
        pltpu.make_async_remote_copy(
            src_ref=pack.at[q], dst_ref=pack.at[q],
            send_sem=pack_send.at[d - 1], recv_sem=pack_recv.at[q],
            device_id={"ia": q}, device_id_type=MESH,
        ).wait_recv()
    both = jnp.concatenate([pack[q] for q in range(n_ia)], axis=0)
    rank_b = both[:, :jl]
    rank_c = both[:, jl:]

    gc[ka] = dot3(rank_c, rank_c, NT)
    grams = []
    for d in range(1, n_ka):
        copy = pltpu.make_async_remote_copy(
            src_ref=gc.at[ka], dst_ref=gc.at[ka],
            send_sem=gc_send.at[d - 1], recv_sem=gc_recv.at[ka],
            device_id={"ka": lax.rem(ka + d, n_ka)}, device_id_type=MESH,
        )
        copy.start()
        grams.append(copy)

    bh, bl = split(rank_b)
    lhs = jnp.concatenate([bh, bl], axis=0)
    lane = lax.broadcasted_iota(jnp.int32, rank_c.shape, 1)

    def planes_of(g, total):
        columns = pl.ds(pl.multiple_of(g * (step * il), il), step * il)
        wide = dot(lhs, th[:, columns])
        inner = wide[:ranks] + (wide[ranks:] + dot(bh, tl[:, columns]))
        for u in range(step):
            column = jnp.sum(
                jnp.where(lane == g * step + u, rank_c, 0.0), axis=1, keepdims=True
            )
            total = total + inner[:, u * il : (u + 1) * il] * column
        return total

    total = lax.fori_loop(0, groups - 1, planes_of, jnp.zeros((ranks, il), F32))

    narrow = dot(lhs, bh, NT)
    gram_b = narrow[:ranks] + (narrow[ranks:] + dot(bh, bl, NT))
    own_a.wait()
    for d in range(1, n_ka):
        q = lax.rem(ka + n_ka - d, n_ka)
        pltpu.make_async_remote_copy(
            src_ref=gc.at[q], dst_ref=gc.at[q],
            send_sem=gc_send.at[d - 1], recv_sem=gc_recv.at[q],
            device_id={"ka": q}, device_id_type=MESH,
        ).wait_recv()
    gram_c = gc[0]
    for q in range(1, n_ka):
        gram_c = gram_c + gc[q]
    share = jnp.concatenate([a_v[q] for q in range(n_ka)], axis=0)
    total = total - dot3(gram_b * gram_c, share)
    total = planes_of(groups - 1, total)

    for kk in range(n_ka):
        for jj in range(n_ja):
            low = kk * ra + jj * rows
            part[jj * n_ka + kk] = total[low : low + rows]

    def scatter(d):
        peer = lax.rem(me + d, n_red)
        return pltpu.make_async_remote_copy(
            src_ref=part.at[peer], dst_ref=recv.at[me],
            send_sem=rs_send.at[d - 1], recv_sem=rs_recv.at[me],
            device_id={"ja": peer // n_ka, "ka": lax.rem(peer, n_ka)}, device_id_type=MESH,
        )

    @pl.loop(1, n_red)
    def _(d):
        scatter(d).start()

    def gather_sum(d, summed):
        q = lax.rem(me + n_red - d, n_red)
        pltpu.make_async_remote_copy(
            src_ref=part.at[q], dst_ref=recv.at[q],
            send_sem=rs_send.at[d - 1], recv_sem=rs_recv.at[q],
            device_id={"ja": q // n_ka, "ka": lax.rem(q, n_ka)}, device_id_type=MESH,
        ).wait_recv()
        return summed + recv[q]

    summed = lax.fori_loop(1, n_red, gather_sum, part[me])

    out_ref[ja] = summed
    spreads = []
    for d in range(1, n_ja):
        copy = pltpu.make_async_remote_copy(
            src_ref=out_ref.at[ja], dst_ref=out_ref.at[ja],
            send_sem=ag_send.at[d - 1], recv_sem=ag_recv.at[ja],
            device_id={"ja": lax.rem(ja + d, n_ja)}, device_id_type=MESH,
        )
        copy.start()
        spreads.append(copy)
    for copy in gathers + grams:
        copy.wait_send()

    @pl.loop(1, n_red)
    def _(d):
        scatter(d).wait_send()

    for d in range(1, n_ja):
        q = lax.rem(ja + n_ja - d, n_ja)
        pltpu.make_async_remote_copy(
            src_ref=out_ref.at[q], dst_ref=out_ref.at[q],
            send_sem=ag_send.at[d - 1], recv_sem=ag_recv.at[q],
            device_id={"ja": q}, device_id_type=MESH,
        ).wait_recv()
    for copy in spreads:
        copy.wait_send()


def local(sizes, tensor, factor_a, factor_b, factor_c):
    n_ia, n_ja, n_ka = sizes
    planes, jl, il = tensor.shape
    ra, rb = factor_a.shape[0], factor_b.shape[0]
    ranks = rb * n_ia
    rows = ra // n_ja
    n_red = n_ja * n_ka
    groups = 4
    wide_c = -(-planes // 128) * 128
    dma = pltpu.SemaphoreType.DMA
    out = pl.pallas_call(
        functools.partial(kernel, n_ia, n_ja, n_ka, groups),
        out_shape=pltpu.VMEM((n_ja, rows, il), F32),
        in_specs=[pl.BlockSpec(memory_space=pl.ANY)] * 4,
        out_specs=pl.BlockSpec(memory_space=pltpu.VMEM),
        scratch_shapes=[
            pltpu.VMEM((planes, jl, il), F32),
            pltpu.VMEM((jl, planes * il), BF16),
            pltpu.VMEM((jl, planes * il), BF16),
            pltpu.VMEM((n_ia, rb, jl + wide_c), F32),
            pltpu.VMEM((rb, planes), F32),
            pltpu.VMEM((n_ka, ra, il), F32),
            pltpu.VMEM((n_ka, ranks, ranks), F32),
            pltpu.VMEM((n_red, rows, il), F32),
            pltpu.VMEM((n_red, rows, il), F32),
            dma((groups,)),
            dma((3,)),
            dma((n_ia,)),
            dma((n_ia,)),
            dma((n_ka,)),
            dma((n_ka,)),
            dma((n_red,)),
            dma((n_red,)),
            dma((n_ja,)),
            dma((n_ja,)),
        ],
        compiler_params=pltpu.CompilerParams(
            collective_id=0, has_side_effects=True, vmem_limit_bytes=56 * 2**20
        ),
        cost_estimate=pl.CostEstimate(
            flops=6 * ranks * planes * jl * il,
            bytes_accessed=4 * planes * jl * il,
            transcendentals=0,
        ),
    )(tensor, factor_a, factor_b, factor_c)
    return out.reshape(ra, il)


def solution(mesh):
    sizes = tuple(mesh.shape[name] for name in ("ia", "ja", "ka"))
    in_specs = (P("ka", "ja", "ia"), P("ka", "ia"), P("ia", "ja"), P("ia", "ka"))
    return jax.shard_map(
        functools.partial(local, sizes), mesh=mesh, in_specs=in_specs,
        out_specs=P("ka", "ia"), check_vma=False,
    )
```

```python
import functools

import jax
import jax.numpy as jnp
from jax import lax
from jax.experimental import pallas as pl
from jax.experimental.pallas import tpu as pltpu
from jax.sharding import PartitionSpec as P

MESH = pl.DeviceIdType.MESH
F32 = jnp.float32
BF16 = jnp.bfloat16
NN = (((1,), (0,)), ((), ()))
NT = (((1,), (1,)), ((), ()))


def split(x):
    high = x.astype(BF16)
    return high, (x - high.astype(F32)).astype(BF16)


def dot(x, y, dims=NN):
    return lax.dot_general(x, y, dims, preferred_element_type=F32)


def dot3(x, y, dims=NN):
    xh, xl = split(x)
    yh, yl = split(y)
    return dot(xh, yh, dims) + (dot(xh, yl, dims) + dot(xl, yh, dims))


def kernel(
    n_ia, n_ja, n_ka, groups,
    t_hbm, a_hbm, b_hbm, c_hbm, out_ref,
    t_v, th, tl, pack, c_v, a_v, gc, part, recv,
    t_sem, loc_sem, pack_send, pack_recv, gc_send, gc_recv,
    red_send, red_recv,
):
    ia, ja, ka = lax.axis_index("ia"), lax.axis_index("ja"), lax.axis_index("ka")
    planes, jl, il = t_v.shape
    rb = pack.shape[1]
    ranks = rb * n_ia
    ra = a_v.shape[1]
    halves, hw = part.shape[0], part.shape[3]
    n_red = n_ja * n_ka
    me = ja * n_ka + ka
    step = planes // groups

    barrier = pltpu.get_barrier_semaphore()
    for d in range(1, n_ia):
        pl.semaphore_signal(
            barrier, inc=1, device_id={"ia": lax.rem(ia + d, n_ia)}, device_id_type=MESH
        )
    @pl.loop(1, n_red)
    def _(d):
        peer = lax.rem(me + d, n_red)
        pl.semaphore_signal(
            barrier, inc=1, device_id={"ja": peer // n_ka, "ka": lax.rem(peer, n_ka)},
            device_id_type=MESH,
        )
    own_b = pltpu.make_async_copy(b_hbm, pack.at[ia, :, pl.ds(0, jl)], loc_sem.at[0])
    own_c = pltpu.make_async_copy(c_hbm, c_v, loc_sem.at[1])
    own_b.start()
    own_c.start()
    loads = []
    for g in range(groups):
        load = pltpu.make_async_copy(
            t_hbm.at[pl.ds(g * step, step)], t_v.at[pl.ds(g * step, step)], t_sem.at[g]
        )
        load.start()
        loads.append(load)
    a_v[...] = jnp.zeros_like(a_v)
    own_a = pltpu.make_async_copy(a_hbm, a_v.at[ka], loc_sem.at[2])
    own_a.start()

    own_c.wait()
    pack[ia, :, jl:] = jnp.concatenate(
        [c_v[...], jnp.zeros((rb, pack.shape[2] - jl - planes), F32)], axis=1
    )
    own_b.wait()
    pl.semaphore_wait(barrier, n_ia - 1 + n_red - 1)

    gathers = []
    for d in range(1, n_ia):
        copy = pltpu.make_async_remote_copy(
            src_ref=pack.at[ia], dst_ref=pack.at[ia],
            send_sem=pack_send.at[d - 1], recv_sem=pack_recv.at[ia],
            device_id={"ia": lax.rem(ia + d, n_ia)}, device_id_type=MESH,
        )
        copy.start()
        gathers.append(copy)

    for g in range(groups):
        loads[g].wait()

        @pl.loop(g * step, (g + 1) * step)
        def _(k):
            high, low = split(t_v[k])
            columns = pl.ds(pl.multiple_of(k * hw, hw), hw)
            for h in range(halves):
                th[h, :, columns] = high[:, h * hw : (h + 1) * hw]
                tl[h, :, columns] = low[:, h * hw : (h + 1) * hw]

    for d in range(1, n_ia):
        q = lax.rem(ia + n_ia - d, n_ia)
        pltpu.make_async_remote_copy(
            src_ref=pack.at[q], dst_ref=pack.at[q],
            send_sem=pack_send.at[d - 1], recv_sem=pack_recv.at[q],
            device_id={"ia": q}, device_id_type=MESH,
        ).wait_recv()
    both = jnp.concatenate([pack[q] for q in range(n_ia)], axis=0)
    rank_b = both[:, :jl]
    rank_c = both[:, jl:]

    gc[ka] = dot3(rank_c, rank_c, NT)
    grams = []
    for d in range(1, n_ka):
        copy = pltpu.make_async_remote_copy(
            src_ref=gc.at[ka], dst_ref=gc.at[ka],
            send_sem=gc_send.at[d - 1], recv_sem=gc_recv.at[ka],
            device_id={"ka": lax.rem(ka + d, n_ka)}, device_id_type=MESH,
        )
        copy.start()
        grams.append(copy)

    bh, bl = split(rank_b)
    lhs = jnp.concatenate([bh, bl], axis=0)
    lane = lax.broadcasted_iota(jnp.int32, rank_c.shape, 1)

    narrow = dot(lhs, bh, NT)
    gram_b = narrow[:ranks] + (narrow[ranks:] + dot(bh, bl, NT))

    def exchange(h, d):
        peer = lax.rem(me + d, n_red)
        return pltpu.make_async_remote_copy(
            src_ref=part.at[h, lax.rem(peer, n_ka)], dst_ref=recv.at[h, me],
            send_sem=red_send.at[h, d - 1], recv_sem=red_recv.at[h, me],
            device_id={"ja": peer // n_ka, "ka": lax.rem(peer, n_ka)}, device_id_type=MESH,
        )

    for h in range(halves):

        def planes_of(g, total):
            columns = pl.ds(pl.multiple_of(g * (step * hw), step * hw), step * hw)
            wide = dot(lhs, th[h, :, columns])
            inner = wide[:ranks] + (wide[ranks:] + dot(bh, tl[h, :, columns]))
            for u in range(step):
                column = jnp.sum(
                    jnp.where(lane == g * step + u, rank_c, 0.0), axis=1, keepdims=True
                )
                total = total + inner[:, u * hw : (u + 1) * hw] * column
            return total

        total = lax.fori_loop(0, groups, planes_of, jnp.zeros((ranks, hw), F32))

        if h == 0:
            own_a.wait()
            for d in range(1, n_ka):
                q = lax.rem(ka + n_ka - d, n_ka)
                pltpu.make_async_remote_copy(
                    src_ref=gc.at[q], dst_ref=gc.at[q],
                    send_sem=gc_send.at[d - 1], recv_sem=gc_recv.at[q],
                    device_id={"ka": q}, device_id_type=MESH,
                ).wait_recv()
            gram_c = gc[0]
            for q in range(1, n_ka):
                gram_c = gram_c + gc[q]
            share = jnp.concatenate([a_v[q] for q in range(n_ka)], axis=0)
            correction = dot3(gram_b * gram_c, share)
        total = total - correction[:, h * hw : (h + 1) * hw]

        for kk in range(n_ka):
            part[h, kk] = total[kk * ra : (kk + 1) * ra]

        @pl.loop(1, n_red)
        def _(d):
            exchange(h, d).start()

        recv[h, me] = part[h, ka]

    for copy in gathers + grams:
        copy.wait_send()

    for h in range(halves):

        @pl.loop(1, n_red)
        def _(d):
            q = lax.rem(me + n_red - d, n_red)
            pltpu.make_async_remote_copy(
                src_ref=part.at[h, ka], dst_ref=recv.at[h, q],
                send_sem=red_send.at[h, d - 1], recv_sem=red_recv.at[h, q],
                device_id={"ja": q // n_ka, "ka": lax.rem(q, n_ka)}, device_id_type=MESH,
            ).wait_recv()

        summed = recv[h, 0]
        for q in range(1, n_red):
            summed = summed + recv[h, q]
        out_ref[:, h * hw : (h + 1) * hw] = summed

    for h in range(halves):

        @pl.loop(1, n_red)
        def _(d):
            exchange(h, d).wait_send()


def local(sizes, tensor, factor_a, factor_b, factor_c):
    n_ia, n_ja, n_ka = sizes
    planes, jl, il = tensor.shape
    ra, rb = factor_a.shape[0], factor_b.shape[0]
    ranks = rb * n_ia
    halves = 2
    hw = il // halves
    n_red = n_ja * n_ka
    groups = 4
    wide_c = -(-planes // 128) * 128
    dma = pltpu.SemaphoreType.DMA
    return pl.pallas_call(
        functools.partial(kernel, n_ia, n_ja, n_ka, groups),
        out_shape=pltpu.VMEM((ra, il), F32),
        in_specs=[pl.BlockSpec(memory_space=pl.ANY)] * 4,
        out_specs=pl.BlockSpec(memory_space=pltpu.VMEM),
        scratch_shapes=[
            pltpu.VMEM((planes, jl, il), F32),
            pltpu.VMEM((halves, jl, planes * hw), BF16),
            pltpu.VMEM((halves, jl, planes * hw), BF16),
            pltpu.VMEM((n_ia, rb, jl + wide_c), F32),
            pltpu.VMEM((rb, planes), F32),
            pltpu.VMEM((n_ka, ra, il), F32),
            pltpu.VMEM((n_ka, ranks, ranks), F32),
            pltpu.VMEM((halves, n_ka, ra, hw), F32),
            pltpu.VMEM((halves, n_red, ra, hw), F32),
            dma((groups,)),
            dma((3,)),
            dma((n_ia,)),
            dma((n_ia,)),
            dma((n_ka,)),
            dma((n_ka,)),
            dma((halves, n_red)),
            dma((halves, n_red)),
        ],
        compiler_params=pltpu.CompilerParams(
            collective_id=0, has_side_effects=True, vmem_limit_bytes=56 * 2**20
        ),
        cost_estimate=pl.CostEstimate(
            flops=6 * ranks * planes * jl * il,
            bytes_accessed=4 * planes * jl * il,
            transcendentals=0,
        ),
    )(tensor, factor_a, factor_b, factor_c)


def solution(mesh):
    sizes = tuple(mesh.shape[name] for name in ("ia", "ja", "ka"))
    in_specs = (P("ka", "ja", "ia"), P("ka", "ia"), P("ia", "ja"), P("ia", "ka"))
    return jax.shard_map(
        functools.partial(local, sizes), mesh=mesh, in_specs=in_specs,
        out_specs=P("ka", "ia"), check_vma=False,
    )
```

```python
import functools

import jax
import jax.numpy as jnp
from jax import lax
from jax.experimental import pallas as pl
from jax.experimental.pallas import tpu as pltpu
from jax.sharding import PartitionSpec as P

MESH = pl.DeviceIdType.MESH
F32 = jnp.float32
BF16 = jnp.bfloat16
NN = (((1,), (0,)), ((), ()))
NT = (((1,), (1,)), ((), ()))


def split(x):
    high = x.astype(BF16)
    return high, (x - high.astype(F32)).astype(BF16)


def dot(x, y, dims=NN):
    return lax.dot_general(x, y, dims, preferred_element_type=F32)


def dot3(x, y, dims=NN):
    xh, xl = split(x)
    yh, yl = split(y)
    return dot(xh, yh, dims) + (dot(xh, yl, dims) + dot(xl, yh, dims))


def kernel(
    n_ia, n_ja, n_ka, groups,
    t_hbm, a_hbm, b_hbm, c_hbm, out_ref,
    t_v, th, tl, b_all, c_all, a_all, part, recv,
    t_sem, loc_sem, fac_send, fac_recv, a_send, a_recv,
    red_send, red_recv,
):
    ia, ja, ka = lax.axis_index("ia"), lax.axis_index("ja"), lax.axis_index("ka")
    planes, jl, il = t_v.shape
    ranks = b_all.shape[1] * n_ia
    ra = a_all.shape[1]
    halves, hw = part.shape[0], part.shape[3]
    n_red = n_ja * n_ka
    me = ja * n_ka + ka
    step = planes // groups

    barrier = pltpu.get_barrier_semaphore()
    for d in range(1, n_ia):
        pl.semaphore_signal(
            barrier, inc=1, device_id={"ia": lax.rem(ia + d, n_ia)}, device_id_type=MESH
        )
    @pl.loop(1, n_red)
    def _(d):
        peer = lax.rem(me + d, n_red)
        pl.semaphore_signal(
            barrier, inc=1, device_id={"ja": peer // n_ka, "ka": lax.rem(peer, n_ka)},
            device_id_type=MESH,
        )
    own = [
        pltpu.make_async_copy(b_hbm, b_all.at[ia], loc_sem.at[0]),
        pltpu.make_async_copy(c_hbm, c_all.at[ia], loc_sem.at[1]),
        pltpu.make_async_copy(a_hbm, a_all.at[ka], loc_sem.at[2]),
    ]
    loads = [
        pltpu.make_async_copy(
            t_hbm.at[pl.ds(g * step, step)], t_v.at[pl.ds(g * step, step)], t_sem.at[g]
        )
        for g in range(groups)
    ]
    for load in own + loads:
        load.start()
    pl.semaphore_wait(barrier, n_ia - 1 + n_red - 1)

    def factors(to, source, sem):
        return [
            pltpu.make_async_remote_copy(
                src_ref=src, dst_ref=dst.at[source],
                send_sem=fac_send.at[i, sem], recv_sem=fac_recv.at[i, source],
                device_id={"ia": to}, device_id_type=MESH,
            )
            for i, (src, dst) in enumerate(((b_hbm, b_all), (c_hbm, c_all)))
        ]

    def ranks_a(to, source, sem):
        return pltpu.make_async_remote_copy(
            src_ref=a_hbm, dst_ref=a_all.at[source],
            send_sem=a_send.at[sem], recv_sem=a_recv.at[source],
            device_id={"ka": to}, device_id_type=MESH,
        )

    sent = []
    for d in range(1, n_ia):
        sent += factors(lax.rem(ia + d, n_ia), ia, d - 1)
    for d in range(1, n_ka):
        sent.append(ranks_a(lax.rem(ka + d, n_ka), ka, d - 1))
    for copy in sent:
        copy.start()

    for g in range(groups):
        loads[g].wait()

        @pl.loop(g * step, (g + 1) * step)
        def _(k):
            high, low = split(t_v[k])
            columns = pl.ds(pl.multiple_of(k * hw, hw), hw)
            for h in range(halves):
                th[h, :, columns] = high[:, h * hw : (h + 1) * hw]
                tl[h, :, columns] = low[:, h * hw : (h + 1) * hw]

    for copy in own:
        copy.wait()
    for d in range(1, n_ka):
        q = lax.rem(ka + n_ka - d, n_ka)
        ranks_a(q, q, d - 1).wait_recv()
    for d in range(1, n_ia):
        q = lax.rem(ia + n_ia - d, n_ia)
        for copy in factors(q, q, d - 1):
            copy.wait_recv()
    rank_b = jnp.concatenate([b_all[q] for q in range(n_ia)], axis=0)
    rank_c = jnp.concatenate([c_all[q] for q in range(n_ia)], axis=0)
    share = jnp.concatenate([a_all[q] for q in range(n_ka)], axis=0)

    bh, bl = split(rank_b)
    lhs = jnp.concatenate([bh, bl], axis=0)
    def exchange(h, d):
        peer = lax.rem(me + d, n_red)
        return pltpu.make_async_remote_copy(
            src_ref=part.at[h, lax.rem(peer, n_ka)], dst_ref=recv.at[h, me],
            send_sem=red_send.at[h, d - 1], recv_sem=red_recv.at[h, me],
            device_id={"ja": peer // n_ka, "ka": lax.rem(peer, n_ka)}, device_id_type=MESH,
        )

    for h in range(halves):

        total = jnp.zeros((ranks, hw), F32)
        for g in range(groups):
            columns = pl.ds(g * step * hw, step * hw)
            wide = dot(lhs, th[h, :, columns])
            inner = wide[:ranks] + (wide[ranks:] + dot(bh, tl[h, :, columns]))
            for u in range(step):
                k = g * step + u
                total = total + inner[:, u * hw : (u + 1) * hw] * rank_c[:, k : k + 1]

            if h == 0 and g == 0:
                narrow = dot(lhs, bh, NT)
                gram_b = narrow[:ranks] + (narrow[ranks:] + dot(bh, bl, NT))
                gram_c = dot3(rank_c, rank_c, NT)
                correction = dot3(gram_b * gram_c, share)
        total = total - correction[:, h * hw : (h + 1) * hw]

        for kk in range(n_ka):
            part[h, kk] = total[kk * ra : (kk + 1) * ra]

        @pl.loop(1, n_red)
        def _(d):
            exchange(h, d).start()

        recv[h, me] = part[h, ka]

    for copy in sent:
        copy.wait_send()

    for h in range(halves):

        @pl.loop(1, n_red)
        def _(d):
            q = lax.rem(me + n_red - d, n_red)
            pltpu.make_async_remote_copy(
                src_ref=part.at[h, ka], dst_ref=recv.at[h, q],
                send_sem=red_send.at[h, d - 1], recv_sem=red_recv.at[h, q],
                device_id={"ja": q // n_ka, "ka": lax.rem(q, n_ka)}, device_id_type=MESH,
            ).wait_recv()

        summed = recv[h, 0]
        for q in range(1, n_red):
            summed = summed + recv[h, q]
        out_ref[:, h * hw : (h + 1) * hw] = summed

    for h in range(halves):

        @pl.loop(1, n_red)
        def _(d):
            exchange(h, d).wait_send()


def local(sizes, tensor, factor_a, factor_b, factor_c):
    n_ia, n_ja, n_ka = sizes
    planes, jl, il = tensor.shape
    ra, rb = factor_a.shape[0], factor_b.shape[0]
    ranks = rb * n_ia
    halves = 2
    hw = il // halves
    n_red = n_ja * n_ka
    groups = 4
    dma = pltpu.SemaphoreType.DMA
    return pl.pallas_call(
        functools.partial(kernel, n_ia, n_ja, n_ka, groups),
        out_shape=pltpu.VMEM((ra, il), F32),
        in_specs=[pl.BlockSpec(memory_space=pl.ANY)] * 4,
        out_specs=pl.BlockSpec(memory_space=pltpu.VMEM),
        scratch_shapes=[
            pltpu.VMEM((planes, jl, il), F32),
            pltpu.VMEM((halves, jl, planes * hw), BF16),
            pltpu.VMEM((halves, jl, planes * hw), BF16),
            pltpu.VMEM((n_ia, rb, jl), F32),
            pltpu.VMEM((n_ia, rb, planes), F32),
            pltpu.VMEM((n_ka, ra, il), F32),
            pltpu.VMEM((halves, n_ka, ra, hw), F32),
            pltpu.VMEM((halves, n_red, ra, hw), F32),
            dma((groups,)),
            dma((3,)),
            dma((2, n_ia)),
            dma((2, n_ia)),
            dma((n_ka,)),
            dma((n_ka,)),
            dma((halves, n_red)),
            dma((halves, n_red)),
        ],
        compiler_params=pltpu.CompilerParams(
            collective_id=0, has_side_effects=True, vmem_limit_bytes=56 * 2**20
        ),
        cost_estimate=pl.CostEstimate(
            flops=6 * ranks * planes * jl * il,
            bytes_accessed=4 * planes * jl * il,
            transcendentals=0,
        ),
    )(tensor, factor_a, factor_b, factor_c)


def solution(mesh):
    sizes = tuple(mesh.shape[name] for name in ("ia", "ja", "ka"))
    in_specs = (P("ka", "ja", "ia"), P("ka", "ia"), P("ia", "ja"), P("ia", "ka"))
    return jax.shard_map(
        functools.partial(local, sizes), mesh=mesh, in_specs=in_specs,
        out_specs=P("ka", "ia"), check_vma=False,
    )
```

```python
import functools

import jax
import jax.numpy as jnp
from jax import lax
from jax.experimental import pallas as pl
from jax.experimental.pallas import tpu as pltpu
from jax.sharding import PartitionSpec as P

MESH = pl.DeviceIdType.MESH
F32 = jnp.float32
BF16 = jnp.bfloat16
NN = (((1,), (0,)), ((), ()))
NT = (((1,), (1,)), ((), ()))


def split(x):
    high = x.astype(BF16)
    return high, (x - high.astype(F32)).astype(BF16)


def dot(x, y, dims=NN):
    return lax.dot_general(x, y, dims, preferred_element_type=F32)


def dot3(x, y, dims=NN):
    xh, xl = split(x)
    yh, yl = split(y)
    return dot(xh, yh, dims) + (dot(xh, yl, dims) + dot(xl, yh, dims))


def kernel(
    n_ia, n_ja, n_ka, groups,
    t_hbm, a_hbm, b_hbm, c_hbm, out_ref,
    t_v, th, b_all, c_all, a_all, part, recv,
    t_sem, loc_sem, fac_send, fac_recv, a_send, a_recv,
    red_send, red_recv,
):
    ia, ja, ka = lax.axis_index("ia"), lax.axis_index("ja"), lax.axis_index("ka")
    planes, jl, il = t_v.shape
    ranks = b_all.shape[1] * n_ia
    ra = a_all.shape[1]
    halves, hw = part.shape[0], part.shape[3]
    n_red = n_ja * n_ka
    me = ja * n_ka + ka
    step = planes // groups

    barrier = pltpu.get_barrier_semaphore()
    for d in range(1, n_ia):
        pl.semaphore_signal(
            barrier, inc=1, device_id={"ia": lax.rem(ia + d, n_ia)}, device_id_type=MESH
        )
    @pl.loop(1, n_red)
    def _(d):
        peer = lax.rem(me + d, n_red)
        pl.semaphore_signal(
            barrier, inc=1, device_id={"ja": peer // n_ka, "ka": lax.rem(peer, n_ka)},
            device_id_type=MESH,
        )
    own = [
        pltpu.make_async_copy(b_hbm, b_all.at[ia], loc_sem.at[0]),
        pltpu.make_async_copy(c_hbm, c_all.at[ia], loc_sem.at[1]),
        pltpu.make_async_copy(a_hbm, a_all.at[ka], loc_sem.at[2]),
    ]
    loads = [
        pltpu.make_async_copy(
            t_hbm.at[pl.ds(g * step, step)], t_v.at[pl.ds(g * step, step)], t_sem.at[g]
        )
        for g in range(groups)
    ]
    for load in own + loads:
        load.start()
    pl.semaphore_wait(barrier, n_ia - 1 + n_red - 1)

    def factors(to, source, sem):
        return [
            pltpu.make_async_remote_copy(
                src_ref=src, dst_ref=dst.at[source],
                send_sem=fac_send.at[i, sem], recv_sem=fac_recv.at[i, source],
                device_id={"ia": to}, device_id_type=MESH,
            )
            for i, (src, dst) in enumerate(((b_hbm, b_all), (c_hbm, c_all)))
        ]

    def ranks_a(to, source, sem):
        return pltpu.make_async_remote_copy(
            src_ref=a_hbm, dst_ref=a_all.at[source],
            send_sem=a_send.at[sem], recv_sem=a_recv.at[source],
            device_id={"ka": to}, device_id_type=MESH,
        )

    sent = []
    for d in range(1, n_ia):
        sent += factors(lax.rem(ia + d, n_ia), ia, d - 1)
    for d in range(1, n_ka):
        sent.append(ranks_a(lax.rem(ka + d, n_ka), ka, d - 1))
    for copy in sent:
        copy.start()

    for g in range(groups):
        loads[g].wait()

        @pl.loop(g * step, (g + 1) * step)
        def _(k):
            high, low = split(t_v[k].T)
            place = pl.ds(pl.multiple_of(k * hw, hw), hw)
            for h in range(halves):
                th[h, place, :jl] = high[h * hw : (h + 1) * hw]
                th[h, place, jl:] = low[h * hw : (h + 1) * hw]

    for copy in own:
        copy.wait()
    for d in range(1, n_ka):
        q = lax.rem(ka + n_ka - d, n_ka)
        ranks_a(q, q, d - 1).wait_recv()
    for d in range(1, n_ia):
        q = lax.rem(ia + n_ia - d, n_ia)
        for copy in factors(q, q, d - 1):
            copy.wait_recv()
    rank_b = jnp.concatenate([b_all[q] for q in range(n_ia)], axis=0)
    rank_c = jnp.concatenate([c_all[q] for q in range(n_ia)], axis=0)
    share = jnp.concatenate([a_all[q] for q in range(n_ka)], axis=0)

    bh, bl = split(rank_b)
    lhs = jnp.concatenate([bh, bl], axis=0)
    stands = jnp.concatenate(
        [lhs, jnp.concatenate([bh, jnp.zeros_like(bl)], axis=0)], axis=1
    )
    twice = jnp.concatenate([rank_c, rank_c], axis=0)
    twice = jnp.concatenate(
        [twice, jnp.zeros((2 * ranks, 128 - planes), F32)], axis=1
    ).T

    def exchange(h, d):
        peer = lax.rem(me + d, n_red)
        return pltpu.make_async_remote_copy(
            src_ref=part.at[h, lax.rem(peer, n_ka)], dst_ref=recv.at[h, me],
            send_sem=red_send.at[h, d - 1], recv_sem=red_recv.at[h, me],
            device_id={"ja": peer // n_ka, "ka": lax.rem(peer, n_ka)}, device_id_type=MESH,
        )

    for h in range(halves):

        flipped = jnp.zeros((hw, 2 * ranks), F32)
        for g in range(groups):
            wide = dot(th[h, pl.ds(g * step * hw, step * hw), :], stands, NT)
            for u in range(step):
                k = g * step + u
                flipped = flipped + wide[u * hw : (u + 1) * hw] * twice[k : k + 1]

            if h == 0 and g == 0:
                narrow = dot(lhs, bh, NT)
                gram_b = narrow[:ranks] + (narrow[ranks:] + dot(bh, bl, NT))
                gram_c = dot3(rank_c, rank_c, NT)
                correction = dot3(gram_b * gram_c, share)
        total = flipped.T
        total = total[:ranks] + total[ranks:] - correction[:, h * hw : (h + 1) * hw]

        for kk in range(n_ka):
            part[h, kk] = total[kk * ra : (kk + 1) * ra]

        @pl.loop(1, n_red)
        def _(d):
            exchange(h, d).start()

        recv[h, me] = part[h, ka]

    for copy in sent:
        copy.wait_send()

    for h in range(halves):

        @pl.loop(1, n_red)
        def _(d):
            q = lax.rem(me + n_red - d, n_red)
            pltpu.make_async_remote_copy(
                src_ref=part.at[h, ka], dst_ref=recv.at[h, q],
                send_sem=red_send.at[h, d - 1], recv_sem=red_recv.at[h, q],
                device_id={"ja": q // n_ka, "ka": lax.rem(q, n_ka)}, device_id_type=MESH,
            ).wait_recv()

        summed = recv[h, 0]
        for q in range(1, n_red):
            summed = summed + recv[h, q]
        out_ref[:, h * hw : (h + 1) * hw] = summed

    for h in range(halves):

        @pl.loop(1, n_red)
        def _(d):
            exchange(h, d).wait_send()


def local(sizes, tensor, factor_a, factor_b, factor_c):
    n_ia, n_ja, n_ka = sizes
    planes, jl, il = tensor.shape
    ra, rb = factor_a.shape[0], factor_b.shape[0]
    ranks = rb * n_ia
    halves = 2
    hw = il // halves
    n_red = n_ja * n_ka
    groups = 4
    dma = pltpu.SemaphoreType.DMA
    return pl.pallas_call(
        functools.partial(kernel, n_ia, n_ja, n_ka, groups),
        out_shape=pltpu.VMEM((ra, il), F32),
        in_specs=[pl.BlockSpec(memory_space=pl.ANY)] * 4,
        out_specs=pl.BlockSpec(memory_space=pltpu.VMEM),
        scratch_shapes=[
            pltpu.VMEM((planes, jl, il), F32),
            pltpu.VMEM((halves, planes * hw, 2 * jl), BF16),
            pltpu.VMEM((n_ia, rb, jl), F32),
            pltpu.VMEM((n_ia, rb, planes), F32),
            pltpu.VMEM((n_ka, ra, il), F32),
            pltpu.VMEM((halves, n_ka, ra, hw), F32),
            pltpu.VMEM((halves, n_red, ra, hw), F32),
            dma((groups,)),
            dma((3,)),
            dma((2, n_ia)),
            dma((2, n_ia)),
            dma((n_ka,)),
            dma((n_ka,)),
            dma((halves, n_red)),
            dma((halves, n_red)),
        ],
        compiler_params=pltpu.CompilerParams(
            collective_id=0, has_side_effects=True, vmem_limit_bytes=56 * 2**20
        ),
        cost_estimate=pl.CostEstimate(
            flops=6 * ranks * planes * jl * il,
            bytes_accessed=4 * planes * jl * il,
            transcendentals=0,
        ),
    )(tensor, factor_a, factor_b, factor_c)


def solution(mesh):
    sizes = tuple(mesh.shape[name] for name in ("ia", "ja", "ka"))
    in_specs = (P("ka", "ja", "ia"), P("ka", "ia"), P("ia", "ja"), P("ia", "ka"))
    return jax.shard_map(
        functools.partial(local, sizes), mesh=mesh, in_specs=in_specs,
        out_specs=P("ka", "ia"), check_vma=False,
    )
```

```python
import functools

import jax
import jax.numpy as jnp
from jax import lax
from jax.experimental import pallas as pl
from jax.experimental.pallas import tpu as pltpu
from jax.sharding import PartitionSpec as P

MESH = pl.DeviceIdType.MESH
F32 = jnp.float32
BF16 = jnp.bfloat16
NN = (((1,), (0,)), ((), ()))
NT = (((1,), (1,)), ((), ()))


def split(x):
    high = x.astype(BF16)
    return high, (x - high.astype(F32)).astype(BF16)


def dot(x, y, dims=NN):
    return lax.dot_general(x, y, dims, preferred_element_type=F32)


def dot3(x, y, dims=NN):
    xh, xl = split(x)
    yh, yl = split(y)
    return dot(xh, yh, dims) + (dot(xh, yl, dims) + dot(xl, yh, dims))


def kernel(
    n_ia, n_ja, n_ka, groups,
    t_hbm, a_hbm, b_hbm, c_hbm, out_ref,
    t_v, th, tl, b_all, c_all, a_all, part, recv,
    t_sem, loc_sem, fac_send, fac_recv, a_send, a_recv,
    red_send, red_recv,
):
    ia, ja, ka = lax.axis_index("ia"), lax.axis_index("ja"), lax.axis_index("ka")
    planes, jl, il = t_v.shape
    ranks = b_all.shape[1] * n_ia
    ra = a_all.shape[1]
    halves, hw = part.shape[0], part.shape[3]
    n_red = n_ja * n_ka
    me = ja * n_ka + ka
    step = planes // groups

    barrier = pltpu.get_barrier_semaphore()
    for d in range(1, n_ia):
        pl.semaphore_signal(
            barrier, inc=1, device_id={"ia": lax.rem(ia + d, n_ia)}, device_id_type=MESH
        )
    @pl.loop(1, n_red)
    def _(d):
        peer = lax.rem(me + d, n_red)
        pl.semaphore_signal(
            barrier, inc=1, device_id={"ja": peer // n_ka, "ka": lax.rem(peer, n_ka)},
            device_id_type=MESH,
        )
    own = [
        pltpu.make_async_copy(b_hbm, b_all.at[ia], loc_sem.at[0]),
        pltpu.make_async_copy(c_hbm, c_all.at[ia], loc_sem.at[1]),
        pltpu.make_async_copy(a_hbm, a_all.at[ka], loc_sem.at[2]),
    ]
    loads = [
        pltpu.make_async_copy(
            t_hbm.at[pl.ds(g * step, step)], t_v.at[pl.ds(g * step, step)], t_sem.at[g]
        )
        for g in range(groups)
    ]
    for load in own + loads:
        load.start()
    pl.semaphore_wait(barrier, n_ia - 1 + n_red - 1)

    def factors(to, source, sem):
        return [
            pltpu.make_async_remote_copy(
                src_ref=src, dst_ref=dst.at[source],
                send_sem=fac_send.at[i, sem], recv_sem=fac_recv.at[i, source],
                device_id={"ia": to}, device_id_type=MESH,
            )
            for i, (src, dst) in enumerate(((b_hbm, b_all), (c_hbm, c_all)))
        ]

    def ranks_a(to, source, sem):
        return pltpu.make_async_remote_copy(
            src_ref=a_hbm, dst_ref=a_all.at[source],
            send_sem=a_send.at[sem], recv_sem=a_recv.at[source],
            device_id={"ka": to}, device_id_type=MESH,
        )

    sent = []
    for d in range(1, n_ia):
        sent += factors(lax.rem(ia + d, n_ia), ia, d - 1)
    for d in range(1, n_ka):
        sent.append(ranks_a(lax.rem(ka + d, n_ka), ka, d - 1))
    for copy in sent:
        copy.start()

    for g in range(groups):
        loads[g].wait()

        @pl.loop(g * step, (g + 1) * step)
        def _(k):
            high, low = split(t_v[k, :, :hw])
            columns = pl.ds(pl.multiple_of(k * hw, hw), hw)
            th[:, columns] = high
            tl[:, columns] = low

    for copy in own:
        copy.wait()
    for d in range(1, n_ka):
        q = lax.rem(ka + n_ka - d, n_ka)
        ranks_a(q, q, d - 1).wait_recv()
    for d in range(1, n_ia):
        q = lax.rem(ia + n_ia - d, n_ia)
        for copy in factors(q, q, d - 1):
            copy.wait_recv()
    rank_b = jnp.concatenate([b_all[q] for q in range(n_ia)], axis=0)
    rank_c = jnp.concatenate([c_all[q] for q in range(n_ia)], axis=0)
    share = jnp.concatenate([a_all[q] for q in range(n_ka)], axis=0)

    bh, bl = split(rank_b)
    lhs = jnp.concatenate([bh, bl], axis=0)
    def exchange(h, d):
        peer = lax.rem(me + d, n_red)
        return pltpu.make_async_remote_copy(
            src_ref=part.at[h, lax.rem(peer, n_ka)], dst_ref=recv.at[h, me],
            send_sem=red_send.at[h, d - 1], recv_sem=red_recv.at[h, me],
            device_id={"ja": peer // n_ka, "ka": lax.rem(peer, n_ka)}, device_id_type=MESH,
        )

    for h in range(halves):

        total = jnp.zeros((ranks, hw), F32)
        for g in range(groups):
            columns = pl.ds(g * step * hw, step * hw)
            if h == 0:
                high, low = th[:, columns], tl[:, columns]
            else:
                high, low = split(
                    jnp.concatenate(
                        [
                            t_v[k, :, h * hw : (h + 1) * hw]
                            for k in range(g * step, (g + 1) * step)
                        ],
                        axis=1,
                    )
                )
            wide = dot(lhs, high)
            inner = wide[:ranks] + (wide[ranks:] + dot(bh, low))
            for u in range(step):
                k = g * step + u
                total = total + inner[:, u * hw : (u + 1) * hw] * rank_c[:, k : k + 1]

            if h == 0 and g == 0:
                narrow = dot(lhs, bh, NT)
                gram_b = narrow[:ranks] + (narrow[ranks:] + dot(bh, bl, NT))
                gram_c = dot3(rank_c, rank_c, NT)
                correction = dot3(gram_b * gram_c, share)
        total = total - correction[:, h * hw : (h + 1) * hw]

        for kk in range(n_ka):
            part[h, kk] = total[kk * ra : (kk + 1) * ra]

        @pl.loop(1, n_red)
        def _(d):
            exchange(h, d).start()

        recv[h, me] = part[h, ka]

    for copy in sent:
        copy.wait_send()

    for h in range(halves):

        @pl.loop(1, n_red)
        def _(d):
            exchange(h, d).wait_send()
            q = lax.rem(me + n_red - d, n_red)
            pltpu.make_async_remote_copy(
                src_ref=part.at[h, ka], dst_ref=recv.at[h, q],
                send_sem=red_send.at[h, d - 1], recv_sem=red_recv.at[h, q],
                device_id={"ja": q // n_ka, "ka": lax.rem(q, n_ka)}, device_id_type=MESH,
            ).wait_recv()

        summed = recv[h, 0]
        for q in range(1, n_red):
            summed = summed + recv[h, q]
        out_ref[:, h * hw : (h + 1) * hw] = summed


def local(sizes, tensor, factor_a, factor_b, factor_c):
    n_ia, n_ja, n_ka = sizes
    planes, jl, il = tensor.shape
    ra, rb = factor_a.shape[0], factor_b.shape[0]
    ranks = rb * n_ia
    halves = 2
    hw = il // halves
    n_red = n_ja * n_ka
    groups = 4
    dma = pltpu.SemaphoreType.DMA
    return pl.pallas_call(
        functools.partial(kernel, n_ia, n_ja, n_ka, groups),
        out_shape=pltpu.VMEM((ra, il), F32),
        in_specs=[pl.BlockSpec(memory_space=pl.ANY)] * 4,
        out_specs=pl.BlockSpec(memory_space=pltpu.VMEM),
        scratch_shapes=[
            pltpu.VMEM((planes, jl, il), F32),
            pltpu.VMEM((jl, planes * hw), BF16),
            pltpu.VMEM((jl, planes * hw), BF16),
            pltpu.VMEM((n_ia, rb, jl), F32),
            pltpu.VMEM((n_ia, rb, planes), F32),
            pltpu.VMEM((n_ka, ra, il), F32),
            pltpu.VMEM((halves, n_ka, ra, hw), F32),
            pltpu.VMEM((halves, n_red, ra, hw), F32),
            dma((groups,)),
            dma((3,)),
            dma((2, n_ia)),
            dma((2, n_ia)),
            dma((n_ka,)),
            dma((n_ka,)),
            dma((halves, n_red)),
            dma((halves, n_red)),
        ],
        compiler_params=pltpu.CompilerParams(
            collective_id=0, has_side_effects=True, vmem_limit_bytes=56 * 2**20
        ),
        cost_estimate=pl.CostEstimate(
            flops=6 * ranks * planes * jl * il,
            bytes_accessed=4 * planes * jl * il,
            transcendentals=0,
        ),
    )(tensor, factor_a, factor_b, factor_c)


def solution(mesh):
    sizes = tuple(mesh.shape[name] for name in ("ia", "ja", "ka"))
    in_specs = (P("ka", "ja", "ia"), P("ka", "ia"), P("ia", "ja"), P("ia", "ka"))
    return jax.shard_map(
        functools.partial(local, sizes), mesh=mesh, in_specs=in_specs,
        out_specs=P("ka", "ia"), check_vma=False,
    )
```

```python
import functools

import jax
import jax.numpy as jnp
from jax import lax
from jax.experimental import pallas as pl
from jax.experimental.pallas import tpu as pltpu
from jax.sharding import PartitionSpec as P

MESH = pl.DeviceIdType.MESH
F32 = jnp.float32
BF16 = jnp.bfloat16
NN = (((1,), (0,)), ((), ()))
NT = (((1,), (1,)), ((), ()))


def split(x):
    high = x.astype(BF16)
    return high, (x - high.astype(F32)).astype(BF16)


def dot(x, y, dims=NN):
    return lax.dot_general(x, y, dims, preferred_element_type=F32)


def dot3(x, y, dims=NN):
    xh, xl = split(x)
    yh, yl = split(y)
    return dot(xh, yh, dims) + (dot(xh, yl, dims) + dot(xl, yh, dims))


def kernel(
    n_ia, n_ja, n_ka, groups,
    t_hbm, a_hbm, b_hbm, c_hbm, out_ref,
    t_v, th, tl, b_all, c_all, a_all, part, recv,
    t_sem, loc_sem, fac_send, fac_recv, a_send, a_recv,
    red_send, red_recv,
):
    ia, ja, ka = lax.axis_index("ia"), lax.axis_index("ja"), lax.axis_index("ka")
    planes, jl, il = t_v.shape
    ranks = b_all.shape[1] * n_ia
    ra = a_all.shape[1]
    halves, hw = part.shape[0], part.shape[3]
    n_red = n_ja * n_ka
    me = ja * n_ka + ka
    step = planes // groups

    barrier = pltpu.get_barrier_semaphore()
    for d in range(1, n_ia):
        pl.semaphore_signal(
            barrier, inc=1, device_id={"ia": lax.rem(ia + d, n_ia)}, device_id_type=MESH
        )
    order = [*range(2, n_red), 1]
    for d in order:
        peer = lax.rem(me + d, n_red)
        pl.semaphore_signal(
            barrier, inc=1, device_id={"ja": peer // n_ka, "ka": lax.rem(peer, n_ka)},
            device_id_type=MESH,
        )

    own = [
        pltpu.make_async_copy(b_hbm, b_all.at[ia], loc_sem.at[0]),
        pltpu.make_async_copy(c_hbm, c_all.at[ia], loc_sem.at[1]),
        pltpu.make_async_copy(a_hbm, a_all.at[ka], loc_sem.at[2]),
    ]
    loads = [
        pltpu.make_async_copy(
            t_hbm.at[pl.ds(g * step, step)], t_v.at[pl.ds(g * step, step)], t_sem.at[g]
        )
        for g in range(groups)
    ]
    for load in own + loads:
        load.start()
    pl.semaphore_wait(barrier, n_ia - 1 + n_red - 1)

    def factors(to, source, sem):
        return [
            pltpu.make_async_remote_copy(
                src_ref=src, dst_ref=dst.at[source],
                send_sem=fac_send.at[i, sem], recv_sem=fac_recv.at[i, source],
                device_id={"ia": to}, device_id_type=MESH,
            )
            for i, (src, dst) in enumerate(((b_hbm, b_all), (c_hbm, c_all)))
        ]

    def ranks_a(to, source, sem):
        return pltpu.make_async_remote_copy(
            src_ref=a_hbm, dst_ref=a_all.at[source],
            send_sem=a_send.at[sem], recv_sem=a_recv.at[source],
            device_id={"ka": to}, device_id_type=MESH,
        )

    sent = []
    for d in range(1, n_ia):
        sent += factors(lax.rem(ia + d, n_ia), ia, d - 1)
    sent = sent[0::2] + sent[1::2]
    for d in range(1, n_ka):
        sent.append(ranks_a(lax.rem(ka + d, n_ka), ka, d - 1))
    for copy in sent:
        copy.start()

    for g in range(groups):
        loads[g].wait()

        @pl.loop(g * step, (g + 1) * step)
        def _(k):
            high, low = split(t_v[k, :, :hw])
            columns = pl.ds(pl.multiple_of(k * hw, hw), hw)
            th[:, columns] = high
            tl[:, columns] = low

    for copy in own:
        copy.wait()
    for d in range(1, n_ka):
        q = lax.rem(ka + n_ka - d, n_ka)
        ranks_a(q, q, d - 1).wait_recv()
    for d in range(1, n_ia):
        q = lax.rem(ia + n_ia - d, n_ia)
        for copy in factors(q, q, d - 1):
            copy.wait_recv()
    rank_b = jnp.concatenate([b_all[q] for q in range(n_ia)], axis=0)
    rank_c = jnp.concatenate([c_all[q] for q in range(n_ia)], axis=0)
    share = jnp.concatenate([a_all[q] for q in range(n_ka)], axis=0)

    bh, bl = split(rank_b)
    lhs = jnp.concatenate([bh, bl], axis=0)
    def exchange(h, d):
        peer = lax.rem(me + d, n_red)
        return pltpu.make_async_remote_copy(
            src_ref=part.at[h, lax.rem(peer, n_ka)], dst_ref=recv.at[h, me],
            send_sem=red_send.at[h, d - 1], recv_sem=red_recv.at[h, me],
            device_id={"ja": peer // n_ka, "ka": lax.rem(peer, n_ka)}, device_id_type=MESH,
        )

    for h in range(halves):

        total = jnp.zeros((ranks, hw), F32)
        for g in range(groups):
            columns = pl.ds(g * step * hw, step * hw)
            if h == 0:
                high, low = th[:, columns], tl[:, columns]
            else:
                pairs = [
                    split(t_v[k, :, h * hw : (h + 1) * hw])
                    for k in range(g * step, (g + 1) * step)
                ]
                high = jnp.concatenate([pair[0] for pair in pairs], axis=1)
                low = jnp.concatenate([pair[1] for pair in pairs], axis=1)
            wide = dot(lhs, high)
            inner = wide[:ranks] + (wide[ranks:] + dot(bh, low))
            for u in range(step):
                k = g * step + u
                total = total + inner[:, u * hw : (u + 1) * hw] * rank_c[:, k : k + 1]

            if h == 0 and g == 0:
                narrow = dot(lhs, bh, NT)
                gram_b = narrow[:ranks] + (narrow[ranks:] + dot(bh, bl, NT))
                gram_c = dot3(rank_c, rank_c, NT)
                correction = dot3(gram_b * gram_c, share)
        total = total - correction[:, h * hw : (h + 1) * hw]

        for kk in range(n_ka):
            part[h, kk] = total[kk * ra : (kk + 1) * ra]

        for d in order:
            exchange(h, d).start()
        recv[h, me] = part[h, ka]

    for copy in sent:
        copy.wait_send()

    for h in range(halves):

        @pl.loop(1, n_red)
        def _(d):
            exchange(h, d).wait_send()
            q = lax.rem(me + n_red - d, n_red)
            pltpu.make_async_remote_copy(
                src_ref=part.at[h, ka], dst_ref=recv.at[h, q],
                send_sem=red_send.at[h, d - 1], recv_sem=red_recv.at[h, q],
                device_id={"ja": q // n_ka, "ka": lax.rem(q, n_ka)}, device_id_type=MESH,
            ).wait_recv()

        summed = recv[h, 0]
        for q in range(1, n_red):
            summed = summed + recv[h, q]
        out_ref[:, h * hw : (h + 1) * hw] = summed


def local(sizes, tensor, factor_a, factor_b, factor_c):
    n_ia, n_ja, n_ka = sizes
    planes, jl, il = tensor.shape
    ra, rb = factor_a.shape[0], factor_b.shape[0]
    ranks = rb * n_ia
    halves = 2
    hw = il // halves
    n_red = n_ja * n_ka
    groups = 8
    dma = pltpu.SemaphoreType.DMA
    return pl.pallas_call(
        functools.partial(kernel, n_ia, n_ja, n_ka, groups),
        out_shape=pltpu.VMEM((ra, il), F32),
        in_specs=[pl.BlockSpec(memory_space=pl.ANY)] * 4,
        out_specs=pl.BlockSpec(memory_space=pltpu.VMEM),
        scratch_shapes=[
            pltpu.VMEM((planes, jl, il), F32),
            pltpu.VMEM((jl, planes * hw), BF16),
            pltpu.VMEM((jl, planes * hw), BF16),
            pltpu.VMEM((n_ia, rb, jl), F32),
            pltpu.VMEM((n_ia, rb, planes), F32),
            pltpu.VMEM((n_ka, ra, il), F32),
            pltpu.VMEM((halves, n_ka, ra, hw), F32),
            pltpu.VMEM((halves, n_red, ra, hw), F32),
            dma((groups,)),
            dma((3,)),
            dma((2, n_ia)),
            dma((2, n_ia)),
            dma((n_ka,)),
            dma((n_ka,)),
            dma((halves, n_red)),
            dma((halves, n_red)),
        ],
        compiler_params=pltpu.CompilerParams(
            collective_id=0, has_side_effects=True, vmem_limit_bytes=56 * 2**20
        ),
        cost_estimate=pl.CostEstimate(
            flops=6 * ranks * planes * jl * il,
            bytes_accessed=4 * planes * jl * il,
            transcendentals=0,
        ),
    )(tensor, factor_a, factor_b, factor_c)


def solution(mesh):
    sizes = tuple(mesh.shape[name] for name in ("ia", "ja", "ka"))
    in_specs = (P("ka", "ja", "ia"), P("ka", "ia"), P("ia", "ja"), P("ia", "ka"))
    return jax.shard_map(
        functools.partial(local, sizes), mesh=mesh, in_specs=in_specs,
        out_specs=P("ka", "ia"), check_vma=False,
    )
```

```python
import functools

import jax
import jax.numpy as jnp
from jax import lax
from jax.experimental import pallas as pl
from jax.experimental.pallas import tpu as pltpu
from jax.sharding import PartitionSpec as P

MESH = pl.DeviceIdType.MESH
F32 = jnp.float32
BF16 = jnp.bfloat16
NN = (((1,), (0,)), ((), ()))
NT = (((1,), (1,)), ((), ()))


def split(x):
    high = x.astype(BF16)
    return high, (x - high.astype(F32)).astype(BF16)


def dot(x, y, dims=NN):
    return lax.dot_general(x, y, dims, preferred_element_type=F32)


def dot3(x, y, dims=NN):
    xh, xl = split(x)
    yh, yl = split(y)
    return dot(xh, yh, dims) + (dot(xh, yl, dims) + dot(xl, yh, dims))


def kernel(
    n_ia, n_ja, n_ka, groups,
    t_hbm, a_hbm, b_hbm, c_hbm, out_ref,
    t_v, th, tl, b_all, c_all, a_all, part, recv,
    t_sem, loc_sem, fac_send, fac_recv, a_send, a_recv,
    red_send, red_recv,
):
    ia, ja, ka = lax.axis_index("ia"), lax.axis_index("ja"), lax.axis_index("ka")
    planes, jl, il = t_v.shape
    ranks = b_all.shape[1] * n_ia
    ra = a_all.shape[1]
    halves, hw = part.shape[0], part.shape[3]
    n_red = n_ja * n_ka
    me = ja * n_ka + ka
    step = planes // groups

    barrier = pltpu.get_barrier_semaphore()
    for d in range(1, n_ia):
        pl.semaphore_signal(
            barrier, inc=1, device_id={"ia": lax.rem(ia + d, n_ia)}, device_id_type=MESH
        )
    @pl.loop(1, n_red)
    def _(d):
        peer = lax.rem(me + d, n_red)
        pl.semaphore_signal(
            barrier, inc=1, device_id={"ja": peer // n_ka, "ka": lax.rem(peer, n_ka)},
            device_id_type=MESH,
        )
    own = [
        pltpu.make_async_copy(b_hbm, b_all.at[ia], loc_sem.at[0]),
        pltpu.make_async_copy(c_hbm, c_all.at[ia], loc_sem.at[1]),
        pltpu.make_async_copy(a_hbm, a_all.at[ka], loc_sem.at[2]),
    ]
    loads = []
    for h in range(halves):
        for g in range(groups):
            place = (pl.ds(g * step, step), slice(None), pl.ds(h * hw, hw))
            loads.append(
                pltpu.make_async_copy(
                    t_hbm.at[place], t_v.at[place], t_sem.at[h * groups + g]
                )
            )
    for load in own + loads[:groups]:
        load.start()
    pl.semaphore_wait(barrier, n_ia - 1 + n_red - 1)

    def factors(to, source, sem):
        return [
            pltpu.make_async_remote_copy(
                src_ref=src, dst_ref=dst.at[source],
                send_sem=fac_send.at[i, sem], recv_sem=fac_recv.at[i, source],
                device_id={"ia": to}, device_id_type=MESH,
            )
            for i, (src, dst) in enumerate(((b_hbm, b_all), (c_hbm, c_all)))
        ]

    def ranks_a(to, source, sem):
        return pltpu.make_async_remote_copy(
            src_ref=a_hbm, dst_ref=a_all.at[source],
            send_sem=a_send.at[sem], recv_sem=a_recv.at[source],
            device_id={"ka": to}, device_id_type=MESH,
        )

    sent = []
    for d in range(1, n_ia):
        sent += factors(lax.rem(ia + d, n_ia), ia, d - 1)
    for d in range(1, n_ka):
        sent.append(ranks_a(lax.rem(ka + d, n_ka), ka, d - 1))
    for copy in sent + loads[groups:]:
        copy.start()

    for g in range(groups):
        loads[g].wait()

        @pl.loop(g * step, (g + 1) * step)
        def _(k):
            high, low = split(t_v[k, :, :hw])
            columns = pl.ds(pl.multiple_of(k * hw, hw), hw)
            th[:, columns] = high
            tl[:, columns] = low

    for copy in own:
        copy.wait()
    for d in range(1, n_ka):
        q = lax.rem(ka + n_ka - d, n_ka)
        ranks_a(q, q, d - 1).wait_recv()
    for d in range(1, n_ia):
        q = lax.rem(ia + n_ia - d, n_ia)
        for copy in factors(q, q, d - 1):
            copy.wait_recv()
    rank_b = jnp.concatenate([b_all[q] for q in range(n_ia)], axis=0)
    rank_c = jnp.concatenate([c_all[q] for q in range(n_ia)], axis=0)
    share = jnp.concatenate([a_all[q] for q in range(n_ka)], axis=0)

    bh, bl = split(rank_b)
    lhs = jnp.concatenate([bh, bl], axis=0)
    def exchange(h, d):
        peer = lax.rem(me + d, n_red)
        return pltpu.make_async_remote_copy(
            src_ref=part.at[h, lax.rem(peer, n_ka)], dst_ref=recv.at[h, me],
            send_sem=red_send.at[h, d - 1], recv_sem=red_recv.at[h, me],
            device_id={"ja": peer // n_ka, "ka": lax.rem(peer, n_ka)}, device_id_type=MESH,
        )

    for h in range(halves):
        if h > 0:
            for load in loads[h * groups : (h + 1) * groups]:
                load.wait()
        total = jnp.zeros((ranks, hw), F32)
        for g in range(groups):
            columns = pl.ds(g * step * hw, step * hw)
            if h == 0:
                high, low = th[:, columns], tl[:, columns]
            else:
                high, low = split(
                    jnp.concatenate(
                        [
                            t_v[k, :, h * hw : (h + 1) * hw]
                            for k in range(g * step, (g + 1) * step)
                        ],
                        axis=1,
                    )
                )
            wide = dot(lhs, high)
            inner = wide[:ranks] + (wide[ranks:] + dot(bh, low))
            for u in range(step):
                k = g * step + u
                total = total + inner[:, u * hw : (u + 1) * hw] * rank_c[:, k : k + 1]

            if h == 0 and g == 0:
                narrow = dot(lhs, bh, NT)
                gram_b = narrow[:ranks] + (narrow[ranks:] + dot(bh, bl, NT))
                gram_c = dot3(rank_c, rank_c, NT)
                correction = dot3(gram_b * gram_c, share)
        total = total - correction[:, h * hw : (h + 1) * hw]

        for kk in range(n_ka):
            part[h, kk] = total[kk * ra : (kk + 1) * ra]

        @pl.loop(1, n_red)
        def _(d):
            exchange(h, d).start()

        recv[h, me] = part[h, ka]

    for copy in sent:
        copy.wait_send()

    for h in range(halves):

        @pl.loop(1, n_red)
        def _(d):
            exchange(h, d).wait_send()
            q = lax.rem(me + n_red - d, n_red)
            pltpu.make_async_remote_copy(
                src_ref=part.at[h, ka], dst_ref=recv.at[h, q],
                send_sem=red_send.at[h, d - 1], recv_sem=red_recv.at[h, q],
                device_id={"ja": q // n_ka, "ka": lax.rem(q, n_ka)}, device_id_type=MESH,
            ).wait_recv()

        summed = recv[h, 0]
        for q in range(1, n_red):
            summed = summed + recv[h, q]
        out_ref[:, h * hw : (h + 1) * hw] = summed


def local(sizes, tensor, factor_a, factor_b, factor_c):
    n_ia, n_ja, n_ka = sizes
    planes, jl, il = tensor.shape
    ra, rb = factor_a.shape[0], factor_b.shape[0]
    ranks = rb * n_ia
    halves = 2
    hw = il // halves
    n_red = n_ja * n_ka
    groups = 4
    dma = pltpu.SemaphoreType.DMA
    return pl.pallas_call(
        functools.partial(kernel, n_ia, n_ja, n_ka, groups),
        out_shape=pltpu.VMEM((ra, il), F32),
        in_specs=[pl.BlockSpec(memory_space=pl.ANY)] * 4,
        out_specs=pl.BlockSpec(memory_space=pltpu.VMEM),
        scratch_shapes=[
            pltpu.VMEM((planes, jl, il), F32),
            pltpu.VMEM((jl, planes * hw), BF16),
            pltpu.VMEM((jl, planes * hw), BF16),
            pltpu.VMEM((n_ia, rb, jl), F32),
            pltpu.VMEM((n_ia, rb, planes), F32),
            pltpu.VMEM((n_ka, ra, il), F32),
            pltpu.VMEM((halves, n_ka, ra, hw), F32),
            pltpu.VMEM((halves, n_red, ra, hw), F32),
            dma((halves * groups,)),
            dma((3,)),
            dma((2, n_ia)),
            dma((2, n_ia)),
            dma((n_ka,)),
            dma((n_ka,)),
            dma((halves, n_red)),
            dma((halves, n_red)),
        ],
        compiler_params=pltpu.CompilerParams(
            collective_id=0, has_side_effects=True, vmem_limit_bytes=56 * 2**20
        ),
        cost_estimate=pl.CostEstimate(
            flops=6 * ranks * planes * jl * il,
            bytes_accessed=4 * planes * jl * il,
            transcendentals=0,
        ),
    )(tensor, factor_a, factor_b, factor_c)


def solution(mesh):
    sizes = tuple(mesh.shape[name] for name in ("ia", "ja", "ka"))
    in_specs = (P("ka", "ja", "ia"), P("ka", "ia"), P("ia", "ja"), P("ia", "ka"))
    return jax.shard_map(
        functools.partial(local, sizes), mesh=mesh, in_specs=in_specs,
        out_specs=P("ka", "ia"), check_vma=False,
    )
```

```python
import functools

import jax
import jax.numpy as jnp
from jax import lax
from jax.experimental import pallas as pl
from jax.experimental.pallas import tpu as pltpu
from jax.sharding import PartitionSpec as P

MESH = pl.DeviceIdType.MESH
F32 = jnp.float32
BF16 = jnp.bfloat16
NN = (((1,), (0,)), ((), ()))
NT = (((1,), (1,)), ((), ()))


def split(x):
    high = x.astype(BF16)
    return high, (x - high.astype(F32)).astype(BF16)


def dot(x, y, dims=NN):
    return lax.dot_general(x, y, dims, preferred_element_type=F32)


def dot3(x, y, dims=NN):
    xh, xl = split(x)
    yh, yl = split(y)
    return dot(xh, yh, dims) + (dot(xh, yl, dims) + dot(xl, yh, dims))


def kernel(
    n_ia, n_ja, n_ka, groups,
    t_hbm, a_hbm, b_hbm, c_hbm, out_ref,
    t_v, th, tl, b_all, c_all, a_all, part, recv,
    t_sem, loc_sem, fac_send, fac_recv, a_send, a_recv,
    red_send, red_recv,
):
    ia, ja, ka = lax.axis_index("ia"), lax.axis_index("ja"), lax.axis_index("ka")
    planes, jl, il = t_v.shape
    ranks = b_all.shape[1] * n_ia
    ra = a_all.shape[1]
    halves, hw = part.shape[0], part.shape[3]
    n_red = n_ja * n_ka
    me = ja * n_ka + ka
    step = planes // groups
    wide_step = 2 * step

    barrier = pltpu.get_barrier_semaphore()
    for d in range(1, n_ia):
        pl.semaphore_signal(
            barrier, inc=1, device_id={"ia": lax.rem(ia + d, n_ia)}, device_id_type=MESH
        )
    @pl.loop(1, n_red)
    def _(d):
        peer = lax.rem(me + d, n_red)
        pl.semaphore_signal(
            barrier, inc=1, device_id={"ja": peer // n_ka, "ka": lax.rem(peer, n_ka)},
            device_id_type=MESH,
        )
    own = [
        pltpu.make_async_copy(b_hbm, b_all.at[ia], loc_sem.at[0]),
        pltpu.make_async_copy(c_hbm, c_all.at[ia], loc_sem.at[1]),
        pltpu.make_async_copy(a_hbm, a_all.at[ka], loc_sem.at[2]),
    ]
    loads = [
        pltpu.make_async_copy(
            t_hbm.at[pl.ds(g * step, step)], t_v.at[pl.ds(g * step, step)], t_sem.at[g]
        )
        for g in range(groups)
    ]
    for load in own + loads:
        load.start()
    pl.semaphore_wait(barrier, n_ia - 1 + n_red - 1)

    def factors(to, source, sem):
        return [
            pltpu.make_async_remote_copy(
                src_ref=src, dst_ref=dst.at[source],
                send_sem=fac_send.at[i, sem], recv_sem=fac_recv.at[i, source],
                device_id={"ia": to}, device_id_type=MESH,
            )
            for i, (src, dst) in enumerate(((b_hbm, b_all), (c_hbm, c_all)))
        ]

    def ranks_a(to, source, sem):
        return pltpu.make_async_remote_copy(
            src_ref=a_hbm, dst_ref=a_all.at[source],
            send_sem=a_send.at[sem], recv_sem=a_recv.at[source],
            device_id={"ka": to}, device_id_type=MESH,
        )

    sent = []
    for d in range(1, n_ia):
        sent += factors(lax.rem(ia + d, n_ia), ia, d - 1)
    for d in range(1, n_ka):
        sent.append(ranks_a(lax.rem(ka + d, n_ka), ka, d - 1))
    for copy in sent:
        copy.start()

    for g in range(groups):
        loads[g].wait()

        @pl.loop(g * step, (g + 1) * step)
        def _(k):
            high, low = split(t_v[k, :, :hw])
            columns = pl.ds(pl.multiple_of(k * hw, hw), hw)
            th[:, columns] = high
            tl[:, columns] = low

    for copy in own:
        copy.wait()
    for d in range(1, n_ka):
        q = lax.rem(ka + n_ka - d, n_ka)
        ranks_a(q, q, d - 1).wait_recv()
    for d in range(1, n_ia):
        q = lax.rem(ia + n_ia - d, n_ia)
        for copy in factors(q, q, d - 1):
            copy.wait_recv()
    rank_b = jnp.concatenate([b_all[q] for q in range(n_ia)], axis=0)
    rank_c = jnp.concatenate([c_all[q] for q in range(n_ia)], axis=0)
    share = jnp.concatenate([a_all[q] for q in range(n_ka)], axis=0)

    bh, bl = split(rank_b)
    lhs = jnp.concatenate([bh, bl], axis=0)
    def exchange(h, d):
        peer = lax.rem(me + d, n_red)
        return pltpu.make_async_remote_copy(
            src_ref=part.at[h, lax.rem(peer, n_ka)], dst_ref=recv.at[h, me],
            send_sem=red_send.at[h, d - 1], recv_sem=red_recv.at[h, me],
            device_id={"ja": peer // n_ka, "ka": lax.rem(peer, n_ka)}, device_id_type=MESH,
        )

    for h in range(halves):

        total = jnp.zeros((ranks, hw), F32)
        for g in range(planes // wide_step):
            columns = pl.ds(g * wide_step * hw, wide_step * hw)
            if h == 0:
                high, low = th[:, columns], tl[:, columns]
            else:
                high, low = split(
                    jnp.concatenate(
                        [
                            t_v[k, :, h * hw : (h + 1) * hw]
                            for k in range(g * wide_step, (g + 1) * wide_step)
                        ],
                        axis=1,
                    )
                )
            wide = dot(lhs, high)
            inner = wide[:ranks] + (wide[ranks:] + dot(bh, low))
            for u in range(wide_step):
                k = g * wide_step + u
                total = total + inner[:, u * hw : (u + 1) * hw] * rank_c[:, k : k + 1]

            if h == 0 and g == 0:
                narrow = dot(lhs, bh, NT)
                gram_b = narrow[:ranks] + (narrow[ranks:] + dot(bh, bl, NT))
                gram_c = dot3(rank_c, rank_c, NT)
                correction = dot3(gram_b * gram_c, share)
        total = total - correction[:, h * hw : (h + 1) * hw]

        for kk in range(n_ka):
            part[h, kk] = total[kk * ra : (kk + 1) * ra]

        @pl.loop(1, n_red)
        def _(d):
            exchange(h, d).start()

        recv[h, me] = part[h, ka]

    for copy in sent:
        copy.wait_send()

    for h in range(halves):

        @pl.loop(1, n_red)
        def _(d):
            exchange(h, d).wait_send()
            q = lax.rem(me + n_red - d, n_red)
            pltpu.make_async_remote_copy(
                src_ref=part.at[h, ka], dst_ref=recv.at[h, q],
                send_sem=red_send.at[h, d - 1], recv_sem=red_recv.at[h, q],
                device_id={"ja": q // n_ka, "ka": lax.rem(q, n_ka)}, device_id_type=MESH,
            ).wait_recv()

        summed = recv[h, 0]
        for q in range(1, n_red):
            summed = summed + recv[h, q]
        out_ref[:, h * hw : (h + 1) * hw] = summed


def local(sizes, tensor, factor_a, factor_b, factor_c):
    n_ia, n_ja, n_ka = sizes
    planes, jl, il = tensor.shape
    ra, rb = factor_a.shape[0], factor_b.shape[0]
    ranks = rb * n_ia
    halves = 2
    hw = il // halves
    n_red = n_ja * n_ka
    groups = 4
    dma = pltpu.SemaphoreType.DMA
    return pl.pallas_call(
        functools.partial(kernel, n_ia, n_ja, n_ka, groups),
        out_shape=pltpu.VMEM((ra, il), F32),
        in_specs=[pl.BlockSpec(memory_space=pl.ANY)] * 4,
        out_specs=pl.BlockSpec(memory_space=pltpu.VMEM),
        scratch_shapes=[
            pltpu.VMEM((planes, jl, il), F32),
            pltpu.VMEM((jl, planes * hw), BF16),
            pltpu.VMEM((jl, planes * hw), BF16),
            pltpu.VMEM((n_ia, rb, jl), F32),
            pltpu.VMEM((n_ia, rb, planes), F32),
            pltpu.VMEM((n_ka, ra, il), F32),
            pltpu.VMEM((halves, n_ka, ra, hw), F32),
            pltpu.VMEM((halves, n_red, ra, hw), F32),
            dma((groups,)),
            dma((3,)),
            dma((2, n_ia)),
            dma((2, n_ia)),
            dma((n_ka,)),
            dma((n_ka,)),
            dma((halves, n_red)),
            dma((halves, n_red)),
        ],
        compiler_params=pltpu.CompilerParams(
            collective_id=0, has_side_effects=True, vmem_limit_bytes=56 * 2**20
        ),
        cost_estimate=pl.CostEstimate(
            flops=6 * ranks * planes * jl * il,
            bytes_accessed=4 * planes * jl * il,
            transcendentals=0,
        ),
    )(tensor, factor_a, factor_b, factor_c)


def solution(mesh):
    sizes = tuple(mesh.shape[name] for name in ("ia", "ja", "ka"))
    in_specs = (P("ka", "ja", "ia"), P("ka", "ia"), P("ia", "ja"), P("ia", "ka"))
    return jax.shard_map(
        functools.partial(local, sizes), mesh=mesh, in_specs=in_specs,
        out_specs=P("ka", "ia"), check_vma=False,
    )
```
